256 devices in a mesh: cap: 64 (over x, z, core), temp: 4 (over y).
Axes of the slice: x: 4, y: 4, z: 8, core: 2. Of those that a mesh axis runs over, the one named last changes fastest.
Arguments:
- value_next: float32 [4096, 128, 384], P('cap', 'temp'), may hold values from -6 to 6
- cap_taps: float32 [63], replicated, may hold values from 0.05 to 0.25
- temp_taps: float32 [63], replicated, may hold values from 0.05 to 0.25
- hazard: float32 [128], P('temp'), may hold values from 0.1 to 0.6
- jump_table: int32 [24], replicated, may hold values from 0 to 23
- band_start: int32 [64], P('cap'), may hold values from 0 to 4000, as said below
- interp_weights: float32 [4096, 768], P('cap'), may hold values from -0.625 to 0.625
- choice_index: int32 [4096, 8], P('cap'), may hold values from 0 to 20
- flow_utility: float32 [4096, 8], P('cap'), may hold values from -1 to 1
- carbon_gain: float32 [384], replicated, may hold values from 0 to 1
- temp_cost: float32 [128], P('temp'), may hold values from 0.2 to 1
Outputs:
- value_new: float32 [4096, 128, 384], P('cap', 'temp')
The draws below stay inside these ranges and needn't reach their ends.
Inputs may be any that keep to these rules, and one draw needn't show every extreme that they name: `band_start`: block p's band begins between p * 64 - 32 and p * 64: block 0's at 0, the last block's at 4000, and every other block's between p * 64 - 31 and p * 64 - 1, so that its band takes rows of both neighbouring blocks.
All inputs are finite; a program needn't handle non-finite values.
Results may differ from the reference program's by a relative error of at most 0.000057.
Values sent between devices are 32-bit elements; how exact they have to be, the bound alone decides.
A program may use at most 128 MiB of HBM per device.

```python
import math
import jax
import jax.numpy as jnp
from jax import lax

S = 24
CK = 64
RADIUS = 31
NC = 8
LEVELS = 21
TAPS = 63
REACH = 32
BAND = 96
NK = 4096
NT = 128
SM = 384
N_CAP = 64


def draw_band_start(key, part):
    key = jax.random.fold_in(key, 11)
    lower_rows = jax.random.randint(key, (N_CAP,), 1, REACH, dtype=jnp.int32)
    blocks = jnp.arange(N_CAP, dtype=jnp.int32)
    starts = blocks * CK - lower_rows
    starts = jnp.where(blocks == 0, 0, starts)
    starts = jnp.where(blocks == N_CAP - 1, NK - BAND, starts)
    return starts.astype(jnp.int32)


def with_ends(entries, own_key, least, largest):
    shape = entries.shape
    place = [jax.random.randint(jax.random.fold_in(own_key, axis), (), 0, shape[axis]) for axis in range(len(shape))]
    entries = entries.at[tuple(place)].set(least)
    longest = shape.index(max(shape))
    place[longest] = (place[longest] + 1) % shape[longest]
    return entries.at[tuple(place)].set(largest)


def block_levels(rng, dims, cuts, least, high):
    level, own = 1.0, jax.random.fold_in(rng, 6)
    for dim, blocks in cuts:
        draws = jnp.exp(jax.random.uniform(jax.random.fold_in(own, dim), (blocks,), jnp.float32, least / len(cuts), high / len(cuts)))
        level = level * jnp.repeat(draws, dims[dim] // blocks).reshape([-1 if axis == dim else 1 for axis in range(len(dims))])
    return level


def bell_draw(rng, dims, scale, limit, split=(), held_as=jnp.bfloat16):
    array = scale * jax.random.normal(rng, dims, jnp.float32)
    if split:
        array = array * block_levels(rng, dims, split, -0.22, 0.18)
    return jnp.clip(array, -limit, limit).astype(held_as)


def setup_inputs(seed: int = 0) -> dict:
    arg_keys = jax.random.split(jax.random.key(seed), 12)
    return {
        "value_next": bell_draw(arg_keys[0], (NK, NT, SM), 1.0, 6.0, ((0, 64), (1, 4)), jnp.float32),
        "cap_taps": jnp.clip(jnp.exp(jax.random.uniform(arg_keys[1], (TAPS,), jnp.float32, math.log(0.05), math.log(0.25))), 0.05, 0.25),
        "temp_taps": jnp.clip(jnp.exp(jax.random.uniform(arg_keys[2], (TAPS,), jnp.float32, math.log(0.05), math.log(0.25))), 0.05, 0.25),
        "hazard": jnp.clip(0.1 + 0.5 * jax.random.uniform(arg_keys[3], (NT,), jnp.float32) ** block_levels(arg_keys[3], (NT,), ((0, 4),), -0.2, 0.2), 0.1, 0.6),
        "jump_table": with_ends(jax.random.randint(arg_keys[4], (S,), 0, S), jax.random.fold_in(arg_keys[4], 1), 0, S - 1).astype(jnp.int32),
        "band_start": draw_band_start(jax.random.fold_in(arg_keys[11], 71), 0),
        "interp_weights": bell_draw(arg_keys[6], (NK, NC * BAND), BAND ** -0.5, 0.625, ((0, 64),), jnp.float32),
        "choice_index": with_ends(jax.random.randint(arg_keys[7], (NK, NC), 0, LEVELS), jax.random.fold_in(arg_keys[7], 1), 0, LEVELS - 1).astype(jnp.int32),
        "flow_utility": jnp.clip(jax.random.uniform(arg_keys[8], (NK, NC), jnp.float32, -1.0, 1.0) * block_levels(arg_keys[8], (NK, NC), ((0, 64),), -0.4, 0.0), -1.0, 1.0),
        "carbon_gain": jnp.clip(jax.random.uniform(arg_keys[9], (SM,), jnp.float32, 0.0, 1.0), 0.0, 1.0),
        "temp_cost": jnp.clip(0.2 + 0.8 * jax.random.uniform(arg_keys[10], (NT,), jnp.float32) ** block_levels(arg_keys[10], (NT,), ((0, 4),), -0.2, 0.2), 0.2, 1.0),
    }


PRECISE = lax.Precision.HIGHEST
DISCOUNT = 0.96


def toeplitz(tap_values, out_first, in_first, out_count, in_count):
    half_width = (tap_values.shape[0] - 1) // 2
    row_index = out_first + lax.broadcasted_iota(jnp.int32, (out_count, in_count), 0)
    col_index = in_first + lax.broadcasted_iota(jnp.int32, (out_count, in_count), 1)
    tap_index = col_index - row_index + half_width
    selector = (tap_index[:, :, None] == jnp.arange(tap_values.shape[0], dtype=jnp.int32)[None, None, :]).astype(jnp.float32)
    return jnp.einsum("ijd,d->ij", selector, tap_values, precision=PRECISE)


def section_mix(expect, hazard, jump_table):
    section_count = jump_table.shape[0]
    row_count, col_count, width_all = expect.shape
    by_section = expect.reshape(row_count, col_count, section_count, width_all // section_count)
    jumped = by_section[:, :, jump_table, :].reshape(row_count, col_count, width_all)
    hazard_rate = hazard[None, :, None]
    return (1.0 - hazard_rate) * expect + hazard_rate * jumped


def reference(value_next, cap_taps, temp_taps, hazard, jump_table, band_start, interp_weights, choice_index, flow_utility, carbon_gain, temp_cost):
    temp_table = toeplitz(temp_taps, 0, 0, NT, NT)
    smooth_t = jnp.einsum("ts,ksc->ktc", temp_table, value_next, precision=PRECISE)
    padded = jnp.pad(smooth_t, ((RADIUS, RADIUS), (0, 0), (0, 0)))
    cap_table = toeplitz(cap_taps, 0, -RADIUS, 64, 64 + 2 * RADIUS)

    def cap_block(block_index):
        piece_rows = lax.dynamic_slice_in_dim(padded, block_index * 64, 64 + 2 * RADIUS, 0)
        return jnp.einsum("kj,jtc->ktc", cap_table, piece_rows, precision=PRECISE)

    expect = lax.map(cap_block, jnp.arange(NK // 64, dtype=jnp.int32)).reshape(NK, NT, SM)
    mixed = section_mix(expect, hazard, jump_table)
    levels = choice_index.astype(jnp.float32) / (LEVELS - 1)
    weights_all = interp_weights.reshape(NK, NC, BAND)

    def landing(block_index):
        start_row = band_start[block_index]
        window = lax.dynamic_slice_in_dim(mixed, start_row, BAND, 0)
        first_row = block_index * CK
        weights = lax.dynamic_slice_in_dim(weights_all, first_row, CK, 0)
        landed = jnp.einsum("kji,itc->kjtc", weights, window, precision=PRECISE)
        level_part = lax.dynamic_slice_in_dim(levels, first_row, CK, 0)[:, :, None, None]
        flow_part = lax.dynamic_slice_in_dim(flow_utility, first_row, CK, 0)[:, :, None, None]
        scores = flow_part + level_part * carbon_gain[None, None, None, :] - level_part * level_part * temp_cost[None, None, :, None] + DISCOUNT * landed
        return jnp.max(scores, axis=1)

    return lax.map(landing, jnp.arange(N_CAP, dtype=jnp.int32)).reshape(NK, NT, SM)
```

```python
import functools

import jax
import jax.numpy as jnp
from jax import lax
from jax.experimental import pallas as pl
from jax.experimental.pallas import tpu as pltpu
from jax.sharding import PartitionSpec as P

RADIUS = 31
TAPS = 63
LEVELS = 21
DISCOUNT = 0.96
GROUP = 8
PACKED = GROUP * RADIUS
FIRST = 24
SECOND = RADIUS - FIRST
SLOTS = 4
EARLY = 5
FIRST_PASS = 3
BLOCK = 80
WIDE = 256
MESH = pl.DeviceIdType.MESH
F32 = jnp.float32
BF16 = jnp.bfloat16


def iota(shape, axis):
    return lax.broadcasted_iota(jnp.int32, shape, axis)


def rounded(x):
    return x.astype(BF16).astype(F32)


def halves(x):
    high = x.astype(BF16)
    return high, (x - high.astype(F32)).astype(BF16)


def mm(a, b):
    return jnp.dot(a, b, preferred_element_type=F32)


def count_steps(x, step, most):
    total = jnp.zeros_like(x)
    for i in range(1, most + 1):
        total = total + jnp.where(x >= step * i, 1, 0)
    return total


def lookup(taps_ref, index):
    found = jnp.zeros(index.shape, F32)
    for d in range(TAPS):
        found = jnp.where(index == d, taps_ref[d], found)
    return found


def stacked_map(q, first_group, groups):
    n = groups * 3 * GROUP
    w = q - n * count_steps(q, n, 2)
    g = count_steps(w, 3 * GROUP, groups - 1)
    u = w - 3 * GROUP * g
    side = count_steps(u, GROUP, 2)
    row = side * 64 + (g + first_group) * GROUP + (u - GROUP * side)
    return jnp.where(q < 3 * n, row, -1000)


def kernel(
    n_cap,
    n_temp,
    v_hbm,
    cap_taps_hbm,
    temp_taps_hbm,
    hazard_hbm,
    jump_table_hbm,
    band_start,
    iw_hbm,
    ci_hbm,
    fu_hbm,
    gain_hbm,
    temp_cost_hbm,
    out,
    cap_taps,
    temp_taps,
    hazard,
    jump_table,
    temp_cost,
    v,
    send_up,
    send_down,
    got_low,
    got_high,
    low_a,
    high_a,
    low_b,
    high_b,
    up_b,
    down_b,
    xt,
    acc,
    stage,
    iw,
    ci,
    fu,
    gain,
    a_mats,
    a_tail,
    a_final,
    jump_mat,
    w2,
    w2p,
    g_early,
    g_second,
    g_late,
    rhs_late,
    ext_base,
    local_sem,
    y_send,
    y_recv,
    k_send,
    k_recv,
):
    p = lax.axis_index("cap")
    b = lax.axis_index("temp")
    cap_rows, temp_rows, cols = v.shape
    groups = cap_rows // GROUP
    last = groups - 1
    has_low, has_high = b > 0, b < n_temp - 1
    has_prev, has_next = p > 0, p < n_cap - 1

    def load(g):
        rows = pl.ds(g * GROUP, GROUP)
        return pltpu.make_async_copy(v_hbm.at[rows], v.at[rows], local_sem.at[g])

    small = [
        pltpu.make_async_copy(src, dst, local_sem.at[groups + i])
        for i, (src, dst) in enumerate(
            (
                (temp_taps_hbm, temp_taps),
                (hazard_hbm, hazard),
                (jump_table_hbm, jump_table),
                (cap_taps_hbm, cap_taps),
                (temp_cost_hbm, temp_cost),
                (iw_hbm, iw),
                (ci_hbm, ci),
                (fu_hbm, fu),
                (gain_hbm, gain),
            )
        )
    ]
    barrier = pltpu.get_barrier_semaphore()
    for there, axis, at in (
        (has_low, "temp", b - 1),
        (has_high, "temp", b + 1),
        (has_prev, "cap", p - 1),
        (has_next, "cap", p + 1),
    ):

        @pl.when(there)
        def _(axis=axis, at=at):
            pl.semaphore_signal(barrier, inc=1, device_id={axis: at}, device_id_type=MESH)

    for g in range(groups):
        load(g).start()
    for copy in small:
        copy.start()

    def going(way, src, dst, slot):
        return pltpu.make_async_remote_copy(
            src_ref=src,
            dst_ref=dst,
            send_sem=y_send.at[way, slot],
            recv_sem=y_recv.at[way, slot],
            device_id={"temp": b + 1 - 2 * way},
            device_id_type=MESH,
        )

    def up(g):
        return going(0, send_up.at[lax.rem(g, SLOTS)], got_low.at[g - 1], g)

    def down(g):
        return going(1, send_down.at[lax.rem(g, SLOTS)], got_high.at[g - 1], g)

    def part_source(part, first):
        if part % 2:
            return None
        source = v_hbm.at[pl.ds(0, GROUP)] if part == 0 else v.at[pl.ds(last * GROUP, GROUP)]
        return source.at[:, pl.ds(first, FIRST), :]

    part_slots = (0, groups, last, groups + 1)

    def up_part(part):
        i = part // 2
        if part % 2 == 0:
            return going(0, part_source(part, SECOND + 1), low_a.at[i], part_slots[part])
        return going(0, up_b.at[i], low_b.at[i], part_slots[part])

    def down_part(part):
        i = part // 2
        if part % 2 == 0:
            return going(1, part_source(part, 0), high_a.at[i], part_slots[part])
        return going(1, down_b.at[i], high_b.at[i], part_slots[part])

    def pack(g):
        load(g).wait()
        slot = lax.rem(g, SLOTS)
        for k in range(GROUP):
            rows = slice(RADIUS * k, RADIUS * (k + 1))
            send_up[slot, rows, :] = v[g * GROUP + k, 1 : RADIUS + 1, :]
            send_down[slot, rows, :] = v[g * GROUP + k, 0:RADIUS, :]

    def y_each(g, do, sending, ways=(up, down)):
        @pl.when(has_high if sending else has_low)
        def _():
            do(ways[0](g))

        @pl.when(has_low if sending else has_high)
        def _():
            do(ways[1](g))

    in_parts = (up_part, down_part)

    def pack_second(i):
        g = i * last
        load(g).wait()
        for k in range(GROUP):
            rows = slice(SECOND * k, SECOND * (k + 1))
            up_b[i, rows, :] = v[g * GROUP + k, 1 : SECOND + 1, :]
            down_b[i, rows, :] = v[g * GROUP + k, FIRST : FIRST + SECOND, :]

    def y_start(g):
        y_each(g, lambda c: c.start(), True)

    def y_wait_send(g):
        y_each(g, lambda c: c.wait_send(), True)

    def y_wait_recv(g):
        y_each(g, lambda c: c.wait_recv(), False)

    neighbours = sum(jnp.where(there, 1, 0) for there in (has_low, has_high, has_prev, has_next))
    pl.semaphore_wait(barrier, neighbours)
    y_each(0, lambda c: c.start(), True, in_parts)
    pack_second(0)
    y_each(1, lambda c: c.start(), True, in_parts)
    pack(1)
    y_start(1)
    for g in range(2, SLOTS + 1):
        pack(g)
    pack_second(1)
    for copy in small[:5]:
        copy.wait()

    @pl.when(jnp.logical_not(has_low))
    def _():
        @pl.loop(0, last - 1)
        def _(g):
            got_low[g] = jnp.zeros((PACKED, cols), F32)

        low_a[...] = jnp.zeros(low_a.shape, F32)
        low_b[...] = jnp.zeros(low_b.shape, F32)

    @pl.when(jnp.logical_not(has_high))
    def _():
        @pl.loop(0, last - 1)
        def _(g):
            got_high[g] = jnp.zeros((PACKED, cols), F32)

        high_a[...] = jnp.zeros(high_a.shape, F32)
        high_b[...] = jnp.zeros(high_b.shape, F32)

    for there, side in ((has_prev, 0), (has_next, 2)):

        @pl.when(jnp.logical_not(there))
        def _(side=side):
            @pl.loop(0, groups)
            def _(g):
                @pl.loop(0, temp_rows)
                def _(t):
                    xt[g, t, side * GROUP : (side + 1) * GROUP, :] = jnp.zeros((GROUP, cols), F32)

    wide = GROUP * temp_rows

    def temperature(high_ref, low_ref, width, blocks):
        t_of = iota((temp_rows, width), 0)
        col = iota((temp_rows, width), 1)
        col8 = iota((GROUP, width), 1)
        index = jnp.full(col.shape, -1, jnp.int32)
        k_of = jnp.full(col8.shape, -1, jnp.int32)
        for q0, per, tap in blocks:
            k = count_steps(col - q0, per, GROUP - 1)
            here = (col >= q0) & (col < q0 + GROUP * per)
            index = jnp.where(here, col - q0 - per * k + tap - t_of, index)
            here = (col8 >= q0) & (col8 < q0 + GROUP * per)
            k_of = jnp.where(here, count_steps(col8 - q0, per, GROUP - 1), k_of)
        found = lookup(temp_taps, index)
        same = k_of == iota((GROUP, width), 0)
        for t in range(0, temp_rows, 2):
            block = jnp.concatenate(
                [jnp.where(same, found[t + i : t + i + 1, :], 0.0) for i in range(2)], axis=0
            )
            high, low = halves(block)
            high_ref[t * GROUP : (t + 2) * GROUP, :] = high
            low_ref[t * GROUP : (t + 2) * GROUP, :] = low

    for m, per, tap in ((0, temp_rows, RADIUS), (1, RADIUS, 0), (2, RADIUS, TAPS)):
        temperature(a_mats.at[2 * m], a_mats.at[2 * m + 1], wide, ((0, per, tap),))
    for m, tap in ((0, SECOND), (1, TAPS)):
        temperature(a_tail.at[2 * m], a_tail.at[2 * m + 1], GROUP * FIRST, ((0, FIRST, tap),))
    temperature(
        a_final.at[0],
        a_final.at[1],
        a_final.shape[2],
        ((0, SECOND, 0), (GROUP * SECOND, SECOND, TAPS + FIRST)),
    )

    lane = iota((GROUP, cols), 1)
    source = lane & 15
    for s in range(cols // 16):
        source = source + jnp.where((lane >> 4) == s, jump_table[s] * 16, 0)

    @pl.loop(0, cols // 16)
    def _(i):
        row = iota((16, cols), 0) + i * 16
        hot = row == jnp.concatenate([source, source], axis=0)
        jump_mat[pl.ds(pl.multiple_of(i * 16, 16), 16), :] = jnp.where(hot, 1.0, 0.0).astype(BF16)

    for copy in small[5:]:
        copy.wait()
    choices = fu.shape[0]
    band = iw.shape[1] // choices
    span = w2.shape[1]
    w2[...] = jnp.zeros(w2.shape, F32)
    for kb in range(groups):
        for j in range(choices):
            w2[(kb * choices + j) * GROUP : (kb * choices + j + 1) * GROUP, 0:band] = iw[
                kb * GROUP : (kb + 1) * GROUP, j * band : (j + 1) * band
            ]
    offset = band_start[0] - p * cap_rows + cap_rows // 2
    place_row = iota((span, span), 0)
    place_col = iota((span, span), 1)
    place = jnp.where((place_col == place_row + offset) & (place_row < band), 1.0, 0.0)
    w2p[...] = DISCOUNT * jnp.dot(
        w2[...], place, precision=lax.Precision.HIGHEST, preferred_element_type=F32
    )

    def landing_matrix(width, blocks):
        def columns(q):
            row = jnp.full(q.shape, -1000, jnp.int32)
            for q0, first, count in blocks:
                row = jnp.where(q >= q0, stacked_map(q - q0, first, count), row)
            return row

        parts = []
        for e0 in range(0, span, 32):
            e = iota((32, width), 0) + e0
            q = iota((32, width), 1)
            parts.append(lookup(cap_taps, columns(q) - e - 1))
        full = jnp.dot(
            w2p[...],
            jnp.concatenate(parts, axis=0),
            precision=lax.Precision.HIGHEST,
            preferred_element_type=F32,
        )
        high = rounded(full)
        q = iota(full.shape, 1)
        low_part = q < 0
        for q0, first, count in blocks:
            n = count * 3 * GROUP
            low_part = low_part | ((q >= q0 + 2 * n) & (q < q0 + 3 * n))
        return jnp.where(low_part, full - high, high)

    ext0 = 9 * GROUP * FIRST_PASS
    g_late[...] = landing_matrix(
        WIDE, tuple((i * BLOCK, EARLY + i, 1) for i in range(groups - EARLY))
    ).astype(BF16)
    g_second[...] = landing_matrix(WIDE, ((0, FIRST_PASS, EARLY - FIRST_PASS),)).astype(BF16)
    w2e = landing_matrix(WIDE, ((0, 0, FIRST_PASS),))
    elane = iota((GROUP, WIDE), 1)
    eye = jnp.where(iota((cap_rows, cap_rows), 0) == iota((cap_rows, cap_rows), 1), 1.0, 0.0)

    def turned(x):
        return lax.dot_general(
            eye,
            x,
            (((1,), (1,)), ((), ())),
            precision=lax.Precision.HIGHEST,
            preferred_element_type=F32,
        )

    flows = turned(fu[...])
    numbers = turned(ci[...].astype(F32))
    for kb in range(groups):
        for j0 in range(0, choices, 2):
            pair = []
            for j in (j0, j0 + 1):
                at = (kb * choices + j) * GROUP
                piece = w2e[at : at + GROUP, :]
                flow = flows[kb * GROUP : (kb + 1) * GROUP, j : j + 1]
                number = numbers[kb * GROUP : (kb + 1) * GROUP, j : j + 1]
                square = number * number
                f1 = rounded(flow)
                f2 = rounded(flow - f1)
                f3 = flow - f1 - f2
                q1 = rounded(square)
                q2 = square - q1
                for i, value in enumerate(
                    (f1, f2, f3, number, number, number, -q1, -q1, -q1, -q2, -q2, -q2)
                ):
                    piece = jnp.where(elane == ext0 + i, value, piece)
                pair.append(piece)
            at = (kb * choices + j0) * GROUP
            g_early[at : at + 2 * GROUP, :] = jnp.concatenate(pair, axis=0).astype(BF16)
    gain_row = gain[...].reshape(1, cols) * (1.0 / (LEVELS - 1))
    g1 = rounded(gain_row)
    g2 = rounded(gain_row - g1)
    g3 = gain_row - g1 - g2
    ext_count = WIDE - ext0
    erow = iota((ext_count, cols), 0)
    base = jnp.where(erow < 3, 1.0, 0.0)
    for i, value in enumerate((g1, g2, g3)):
        base = jnp.where(erow == 3 + i, value, base)
    ext_base[...] = base

    parts = temp_rows // GROUP

    def k_copy(g, ts, slot, to_next):
        src = xt.at[g, ts, GROUP : 2 * GROUP, :]
        side = 0 if to_next else 2
        return pltpu.make_async_remote_copy(
            src_ref=src,
            dst_ref=xt.at[g, ts, side * GROUP : (side + 1) * GROUP, :],
            send_sem=k_send.at[0 if to_next else 1, slot],
            recv_sem=k_recv.at[0 if to_next else 1, slot],
            device_id={"cap": p + 1 if to_next else p - 1},
            device_id_type=MESH,
        )

    def k_each(g, ts, slot, do, sending):
        @pl.when(has_next if sending else has_prev)
        def _():
            do(k_copy(g, ts, slot, True))

        @pl.when(has_prev if sending else has_next)
        def _():
            do(k_copy(g, ts, slot, False))

    every = pl.ds(0, temp_rows)

    def k_start(g):
        k_each(g, every, g, lambda c: c.start(), True)

    def k_wait_recv(g):
        k_each(g, every, g, lambda c: c.wait_recv(), False)

    def k_wait_send(g):
        k_each(g, every, g, lambda c: c.wait_send(), True)

    def part_rows(i):
        return pl.ds(pl.multiple_of(i * GROUP, GROUP), GROUP)

    def term(high_ref, low_ref, rows, x):
        high, low = halves(x)
        a = high_ref[rows, :]
        return mm(a, high) + mm(a, low) + mm(low_ref[rows, :], high)

    def own_term(g):
        x = v[pl.ds(g * GROUP, GROUP)].reshape(wide, cols)
        return term(a_mats.at[0], a_mats.at[1], slice(None), x)

    def mix(g, total, ts):
        high, low = halves(total)
        jumped = mm(high, jump_mat[...]) + mm(low, jump_mat[...])
        for i, t in enumerate(ts):
            rows = slice(i * GROUP, (i + 1) * GROUP)
            h = hazard[t]
            xt[g, t, GROUP : 2 * GROUP, :] = (1.0 - h) * total[rows] + h * jumped[rows]

    def first_part(i, own, lo, hi):
        rows = slice(lo * GROUP, hi * GROUP)
        return (
            own[rows]
            + term(a_tail.at[0], a_tail.at[1], rows, low_a[i].reshape(GROUP * FIRST, cols))
            + term(a_tail.at[2], a_tail.at[3], rows, high_a[i].reshape(GROUP * FIRST, cols))
        )

    def second_part(i, blocks):
        pad = jnp.zeros((a_final.shape[2] - 2 * GROUP * SECOND, cols), F32)
        x = jnp.concatenate([low_b[i], high_b[i], pad], axis=0)
        sums = []
        for lo, hi in blocks:
            sums.append(term(a_final.at[0], a_final.at[1], slice(lo * GROUP, hi * GROUP), x))
        return jnp.concatenate(sums, axis=0)

    def y_step(g):
        pad = jnp.zeros((wide - PACKED, cols), F32)
        total = own_term(g)
        y_wait_recv(g)
        for m, got in ((1, got_low), (2, got_high)):
            x = jnp.concatenate([got[g - 1], pad], axis=0)
            total = total + term(a_mats.at[2 * m], a_mats.at[2 * m + 1], slice(None), x)
        mix(g, total, range(temp_rows))

    def stacked(first_group, count, t):
        x = jnp.concatenate([xt[first_group + i, t] for i in range(count)], axis=0)
        high = rounded(x)
        return [high, x - high, high]

    def early(pair):
        sides = []
        for i in range(2):
            t = pair * 2 + i
            cost = jnp.full((ext_count, cols), temp_cost[t] * (1.0 / ((LEVELS - 1) * (LEVELS - 1))), F32)
            c1 = rounded(cost)
            c2 = rounded(cost - c1)
            c3 = cost - c1 - c2
            ext = ext_base[...]
            for r, value in enumerate((c1, c2, c3, c1, c2, c3)):
                ext = jnp.where(erow == 6 + r, value, ext)
            sides.append(jnp.concatenate(stacked(0, FIRST_PASS, t) + [ext], axis=0).astype(BF16))
        both = jnp.concatenate(sides, axis=1)
        for n in range(3):
            acc[pair, n] = mm(g_early[...], both[:, n * 256 : (n + 1) * 256])

    def second(pair):
        count = EARLY - FIRST_PASS
        pad = jnp.zeros((WIDE - 9 * GROUP * count, cols), F32)
        sides = []
        for i in range(2):
            rows = stacked(FIRST_PASS, count, pair * 2 + i) + [pad]
            sides.append(jnp.concatenate(rows, axis=0).astype(BF16))
        both = jnp.concatenate(sides, axis=1)
        for n in range(3):
            acc[pair, n] += mm(g_second[...], both[:, n * 256 : (n + 1) * 256])

    def build(g, pair):
        pad = jnp.zeros((BLOCK - 9 * GROUP, cols), F32)
        rows = slice((g - EARLY) * BLOCK, (g - EARLY + 1) * BLOCK)
        for i in range(2):
            rhs_late[pair, rows, i * cols : (i + 1) * cols] = jnp.concatenate(
                stacked(g, 1, pair * 2 + i) + [pad], axis=0
            ).astype(BF16)

    def late(pair, slot):
        pad = jnp.zeros((WIDE - (last - EARLY) * BLOCK - 9 * GROUP, cols), F32)
        final = jnp.concatenate(
            [
                jnp.concatenate(stacked(last, 1, pair * 2 + i) + [pad], axis=0).astype(BF16)
                for i in range(2)
            ],
            axis=1,
        )
        both = jnp.concatenate([rhs_late[pair], final], axis=0)
        for n in range(3):
            score = acc[pair, n] + mm(g_late[...], both[:, n * 256 : (n + 1) * 256])
            best = jnp.max(score.reshape(groups, choices, GROUP, 256), axis=1).reshape(cap_rows, 256)
            if n == 0:
                stage[slot, :, 0:256] = best
            elif n == 1:
                stage[slot, :, 256:384] = best[:, 0:128]
                stage[slot + 1, :, 0:128] = best[:, 128:256]
            else:
                stage[slot + 1, :, 128:384] = best

    pairs = temp_rows // 2

    def pair_loop(lo, hi, do):
        @pl.loop(lo, hi, step=2)
        def _(pair):
            do(pair)
            do(pair + 1)

    own = own_term(0)
    for part in range(2):
        y_each(part, lambda c: c.wait_send(), True, in_parts)
    y_start(2)
    for part in range(2):
        y_each(part, lambda c: c.wait_recv(), False, in_parts)
    everywhere = (0, temp_rows)
    mix(0, first_part(0, own, *everywhere) + second_part(0, (everywhere,)), range(temp_rows))
    k_start(0)

    def y_turn(g):
        y_wait_send(g)
        y_start(g + 2)
        y_step(g)
        k_start(g)

    @pl.loop(1, FIRST_PASS)
    def _(g):
        y_turn(g)
        pack(g + SLOTS)

    for done in range(FIRST_PASS):
        if done == FIRST_PASS - 1:
            y_turn(FIRST_PASS)
        k_wait_recv(done)
    pair_loop(0, pairs // 2, early)
    y_turn(EARLY - 1)
    pair_loop(pairs // 2, pairs, early)

    y_wait_send(EARLY)
    y_each(2, lambda c: c.start(), True, in_parts)
    y_step(EARLY)
    k_start(EARLY)
    for done in range(FIRST_PASS, EARLY):
        k_wait_recv(done)
    pair_loop(0, 6, second)
    y_wait_send(EARLY + 1)
    y_step(EARLY + 1)
    k_start(EARLY + 1)
    pair_loop(6, pairs, second)

    def k_part(i):
        k_each(last, part_rows(i), last + i, lambda c: c.start(), True)

    own = own_term(last)
    y_each(3, lambda c: c.start(), True, in_parts)
    y_each(2, lambda c: c.wait_recv(), False, in_parts)
    mix(last, first_part(1, own, 8, 24), range(8, 24))
    k_part(1)
    k_part(2)
    outer = jnp.concatenate([first_part(1, own, 24, 32), first_part(1, own, 0, 8)], axis=0)
    y_each(3, lambda c: c.wait_recv(), False, in_parts)
    mix(last, outer + second_part(1, ((24, 32), (0, 8))), (*range(24, 32), *range(8)))
    k_part(3)
    k_part(0)

    def build_both(pair):
        build(EARLY, pair)
        build(EARLY + 1, pair)

    k_wait_recv(EARLY)
    k_wait_recv(EARLY + 1)
    pair_loop(0, pairs, build_both)

    @pl.loop(0, parts)
    def _(step):
        i = lax.rem(step + 1, parts)
        k_each(last, part_rows(i), last + i, lambda c: c.wait_recv(), False)
        for slot in range(0, GROUP, 2):
            late(i * (GROUP // 2) + slot // 2, slot)
        rows = part_rows(i)
        for kb in range(groups):
            at = slice(kb * GROUP, (kb + 1) * GROUP)
            out[at, rows, :] = jnp.swapaxes(stage[:, at, :], 0, 1)

    for part in range(2, 4):
        y_each(part, lambda c: c.wait_send(), True, in_parts)
    for g in range(last):
        k_wait_send(g)
    for i in range(parts):
        k_each(last, part_rows(i), last + i, lambda c: c.wait_send(), True)


def per_device(n_cap, n_temp, *args):
    value_next, interp_weights = args[0], args[6]
    cap_rows, temp_rows, cols = value_next.shape
    args = list(args)
    args[7], args[8] = args[7].T, args[8].T
    args[0] = pltpu.with_memory_space_constraint(value_next, pltpu.HBM)
    choices = args[8].shape[0]
    groups = cap_rows // GROUP
    rows = cap_rows * choices
    parts = temp_rows // GROUP
    hbm = pl.BlockSpec(memory_space=pl.ANY)
    return pl.pallas_call(
        functools.partial(kernel, n_cap, n_temp),
        out_shape=pltpu.VMEM(value_next.shape, F32),
        in_specs=[hbm] * 5 + [pl.BlockSpec(memory_space=pltpu.SMEM)] + [hbm] * 5,
        out_specs=pl.BlockSpec(memory_space=pltpu.VMEM),
        scratch_shapes=[
            *(pltpu.SMEM(args[i].shape, args[i].dtype) for i in (1, 2, 3, 4)),
            pltpu.SMEM(args[10].shape, F32),
            pltpu.VMEM((cap_rows, temp_rows, cols), F32),
            pltpu.VMEM((SLOTS, PACKED, cols), F32),
            pltpu.VMEM((SLOTS, PACKED, cols), F32),
            pltpu.VMEM((groups - 2, PACKED, cols), F32),
            pltpu.VMEM((groups - 2, PACKED, cols), F32),
            pltpu.VMEM((2, GROUP, FIRST, cols), F32),
            pltpu.VMEM((2, GROUP, FIRST, cols), F32),
            *(pltpu.VMEM((2, GROUP * SECOND, cols), F32) for _ in range(4)),
            pltpu.VMEM((groups, temp_rows, 3 * GROUP, cols), F32),
            pltpu.VMEM((temp_rows // 2, 3, rows, 256), F32),
            pltpu.VMEM((GROUP, cap_rows, cols), F32),
            pltpu.VMEM(interp_weights.shape, F32),
            pltpu.VMEM((choices, cap_rows), jnp.int32),
            pltpu.VMEM((choices, cap_rows), F32),
            pltpu.VMEM((cols,), F32),
            pltpu.VMEM((6, GROUP * temp_rows, GROUP * temp_rows), BF16),
            pltpu.VMEM((4, GROUP * temp_rows, GROUP * FIRST), BF16),
            pltpu.VMEM((2, GROUP * temp_rows, 128), BF16),
            pltpu.VMEM((cols, cols), BF16),
            pltpu.VMEM((rows, 128), F32),
            pltpu.VMEM((rows, 128), F32),
            pltpu.VMEM((rows, WIDE), BF16),
            pltpu.VMEM((rows, WIDE), BF16),
            pltpu.VMEM((rows, WIDE), BF16),
            pltpu.VMEM((temp_rows // 2, (groups - 1 - EARLY) * BLOCK, 2 * cols), BF16),
            pltpu.VMEM((WIDE - 9 * GROUP * FIRST_PASS, cols), F32),
            pltpu.SemaphoreType.DMA((groups + 9,)),
            pltpu.SemaphoreType.DMA((2, groups + 2)),
            pltpu.SemaphoreType.DMA((2, groups + 2)),
            pltpu.SemaphoreType.DMA((2, groups - 1 + parts)),
            pltpu.SemaphoreType.DMA((2, groups - 1 + parts)),
        ],
        compiler_params=pltpu.CompilerParams(
            collective_id=0, has_side_effects=True, vmem_limit_bytes=58 * 1024 * 1024
        ),
        cost_estimate=pl.CostEstimate(flops=6_000_000_000, bytes_accessed=8_000_000, transcendentals=0),
    )(*args)


def solution(mesh):
    in_specs = (
        P("cap", "temp", None),
        P(),
        P(),
        P("temp"),
        P(),
        P("cap"),
        P("cap", None),
        P("cap", None),
        P("cap", None),
        P(),
        P("temp"),
    )
    return jax.shard_map(
        functools.partial(per_device, mesh.shape["cap"], mesh.shape["temp"]),
        mesh=mesh,
        in_specs=in_specs,
        out_specs=P("cap", "temp", None),
        check_vma=False,
    )
```

```python
import functools

import jax
import jax.numpy as jnp
from jax import lax
from jax.experimental import pallas as pl
from jax.experimental.pallas import tpu as pltpu
from jax.sharding import PartitionSpec as P

RADIUS = 31
TAPS = 63
LEVELS = 21
DISCOUNT = 0.96
GROUP = 8
PACKED = GROUP * RADIUS
FIRST = 24
SECOND = RADIUS - FIRST
SLOTS = 4
EARLY = 5
FIRST_PASS = 3
BLOCK = 80
WIDE = 256
MESH = pl.DeviceIdType.MESH
F32 = jnp.float32
BF16 = jnp.bfloat16


def iota(shape, axis):
    return lax.broadcasted_iota(jnp.int32, shape, axis)


def rounded(x):
    return x.astype(BF16).astype(F32)


def halves(x):
    high = x.astype(BF16)
    return high, (x - high.astype(F32)).astype(BF16)


def mm(a, b):
    return jnp.dot(a, b, preferred_element_type=F32)


def count_steps(x, step, most):
    total = jnp.zeros_like(x)
    for i in range(1, most + 1):
        total = total + jnp.where(x >= step * i, 1, 0)
    return total


def lookup(taps_ref, index):
    found = jnp.zeros(index.shape, F32)
    for d in range(TAPS):
        found = jnp.where(index == d, taps_ref[d], found)
    return found


def stacked_map(q, first_group, groups):
    n = groups * 3 * GROUP
    w = q - n * count_steps(q, n, 2)
    g = count_steps(w, 3 * GROUP, groups - 1)
    u = w - 3 * GROUP * g
    side = count_steps(u, GROUP, 2)
    row = side * 64 + (g + first_group) * GROUP + (u - GROUP * side)
    return jnp.where(q < 3 * n, row, -1000)


def kernel(
    n_cap,
    n_temp,
    v_hbm,
    cap_taps_hbm,
    temp_taps_hbm,
    hazard_hbm,
    jump_table_hbm,
    band_start,
    iw_hbm,
    ci_hbm,
    fu_hbm,
    gain_hbm,
    temp_cost_hbm,
    out,
    cap_taps,
    temp_taps,
    hazard,
    jump_table,
    temp_cost,
    v,
    send_up,
    send_down,
    got_low,
    got_high,
    low_a,
    high_a,
    low_b,
    high_b,
    up_b,
    down_b,
    xt,
    acc,
    stage,
    iw,
    ci,
    fu,
    gain,
    a_mats,
    a_tail,
    a_final,
    jump_mat,
    w2,
    w2p,
    g_early,
    g_second,
    g_late,
    rhs_late,
    ext_base,
    local_sem,
    y_send,
    y_recv,
    k_send,
    k_recv,
):
    p = lax.axis_index("cap")
    b = lax.axis_index("temp")
    cap_rows, temp_rows, cols = v.shape
    groups = cap_rows // GROUP
    last = groups - 1
    has_low, has_high = b > 0, b < n_temp - 1
    has_prev, has_next = p > 0, p < n_cap - 1

    def load(g):
        rows = pl.ds(g * GROUP, GROUP)
        return pltpu.make_async_copy(v_hbm.at[rows], v.at[rows], local_sem.at[g])

    small = [
        pltpu.make_async_copy(src, dst, local_sem.at[groups + i])
        for i, (src, dst) in enumerate(
            (
                (temp_taps_hbm, temp_taps),
                (hazard_hbm, hazard),
                (jump_table_hbm, jump_table),
                (cap_taps_hbm, cap_taps),
                (temp_cost_hbm, temp_cost),
                (iw_hbm, iw),
                (ci_hbm, ci),
                (fu_hbm, fu),
                (gain_hbm, gain),
            )
        )
    ]
    barrier = pltpu.get_barrier_semaphore()
    for there, axis, at in (
        (has_low, "temp", b - 1),
        (has_high, "temp", b + 1),
        (has_prev, "cap", p - 1),
        (has_next, "cap", p + 1),
    ):

        @pl.when(there)
        def _(axis=axis, at=at):
            pl.semaphore_signal(barrier, inc=1, device_id={axis: at}, device_id_type=MESH)

    for g in range(groups):
        load(g).start()
    for copy in small:
        copy.start()

    def going(way, src, dst, slot):
        return pltpu.make_async_remote_copy(
            src_ref=src,
            dst_ref=dst,
            send_sem=y_send.at[way, slot],
            recv_sem=y_recv.at[way, slot],
            device_id={"temp": b + 1 - 2 * way},
            device_id_type=MESH,
        )

    def up(g):
        return going(0, send_up.at[lax.rem(g, SLOTS)], got_low.at[g - 1], g)

    def down(g):
        return going(1, send_down.at[lax.rem(g, SLOTS)], got_high.at[g - 1], g)

    def part_source(part, first):
        if part % 2:
            return None
        source = v_hbm.at[pl.ds(0, GROUP)] if part == 0 else v.at[pl.ds(last * GROUP, GROUP)]
        return source.at[:, pl.ds(first, FIRST), :]

    part_slots = (0, groups, last, groups + 1)

    def up_part(part):
        i = part // 2
        if part % 2 == 0:
            return going(0, part_source(part, SECOND + 1), low_a.at[i], part_slots[part])
        return going(0, up_b.at[i], low_b.at[i], part_slots[part])

    def down_part(part):
        i = part // 2
        if part % 2 == 0:
            return going(1, part_source(part, 0), high_a.at[i], part_slots[part])
        return going(1, down_b.at[i], high_b.at[i], part_slots[part])

    def pack(g):
        load(g).wait()
        slot = lax.rem(g, SLOTS)
        for k in range(GROUP):
            rows = slice(RADIUS * k, RADIUS * (k + 1))
            send_up[slot, rows, :] = v[g * GROUP + k, 1 : RADIUS + 1, :]
            send_down[slot, rows, :] = v[g * GROUP + k, 0:RADIUS, :]

    def y_each(g, do, sending, ways=(up, down)):
        @pl.when(has_high if sending else has_low)
        def _():
            do(ways[0](g))

        @pl.when(has_low if sending else has_high)
        def _():
            do(ways[1](g))

    in_parts = (up_part, down_part)

    def pack_second(i):
        g = i * last
        load(g).wait()
        for k in range(GROUP):
            rows = slice(SECOND * k, SECOND * (k + 1))
            up_b[i, rows, :] = v[g * GROUP + k, 1 : SECOND + 1, :]
            down_b[i, rows, :] = v[g * GROUP + k, FIRST : FIRST + SECOND, :]

    def y_start(g):
        y_each(g, lambda c: c.start(), True)

    def y_wait_send(g):
        y_each(g, lambda c: c.wait_send(), True)

    def y_wait_recv(g):
        y_each(g, lambda c: c.wait_recv(), False)

    neighbours = sum(jnp.where(there, 1, 0) for there in (has_low, has_high, has_prev, has_next))
    pl.semaphore_wait(barrier, neighbours)
    y_each(0, lambda c: c.start(), True, in_parts)
    pack_second(0)
    y_each(1, lambda c: c.start(), True, in_parts)
    pack(1)
    y_start(1)
    for g in range(2, SLOTS + 1):
        pack(g)
    pack_second(1)
    for copy in small[:5]:
        copy.wait()

    @pl.when(jnp.logical_not(has_low))
    def _():
        @pl.loop(0, last - 1)
        def _(g):
            got_low[g] = jnp.zeros((PACKED, cols), F32)

        low_a[...] = jnp.zeros(low_a.shape, F32)
        low_b[...] = jnp.zeros(low_b.shape, F32)

    @pl.when(jnp.logical_not(has_high))
    def _():
        @pl.loop(0, last - 1)
        def _(g):
            got_high[g] = jnp.zeros((PACKED, cols), F32)

        high_a[...] = jnp.zeros(high_a.shape, F32)
        high_b[...] = jnp.zeros(high_b.shape, F32)

    for there, side in ((has_prev, 0), (has_next, 2)):

        @pl.when(jnp.logical_not(there))
        def _(side=side):
            @pl.loop(0, groups)
            def _(g):
                @pl.loop(0, temp_rows)
                def _(t):
                    xt[g, t, side * GROUP : (side + 1) * GROUP, :] = jnp.zeros((GROUP, cols), F32)

    wide = GROUP * temp_rows

    def temperature(high_ref, low_ref, width, blocks):
        t_of = iota((temp_rows, width), 0)
        col = iota((temp_rows, width), 1)
        col8 = iota((GROUP, width), 1)
        index = jnp.full(col.shape, -1, jnp.int32)
        k_of = jnp.full(col8.shape, -1, jnp.int32)
        for q0, per, tap in blocks:
            k = count_steps(col - q0, per, GROUP - 1)
            here = (col >= q0) & (col < q0 + GROUP * per)
            index = jnp.where(here, col - q0 - per * k + tap - t_of, index)
            here = (col8 >= q0) & (col8 < q0 + GROUP * per)
            k_of = jnp.where(here, count_steps(col8 - q0, per, GROUP - 1), k_of)
        found = lookup(temp_taps, index)
        same = k_of == iota((GROUP, width), 0)
        for t in range(0, temp_rows, 2):
            block = jnp.concatenate(
                [jnp.where(same, found[t + i : t + i + 1, :], 0.0) for i in range(2)], axis=0
            )
            high, low = halves(block)
            high_ref[t * GROUP : (t + 2) * GROUP, :] = high
            low_ref[t * GROUP : (t + 2) * GROUP, :] = low

    for m, per, tap in ((0, temp_rows, RADIUS), (1, RADIUS, 0), (2, RADIUS, TAPS)):
        temperature(a_mats.at[2 * m], a_mats.at[2 * m + 1], wide, ((0, per, tap),))
    for m, tap in ((0, SECOND), (1, TAPS)):
        temperature(a_tail.at[2 * m], a_tail.at[2 * m + 1], GROUP * FIRST, ((0, FIRST, tap),))
    temperature(
        a_final.at[0],
        a_final.at[1],
        a_final.shape[2],
        ((0, SECOND, 0), (GROUP * SECOND, SECOND, TAPS + FIRST)),
    )

    lane = iota((GROUP, cols), 1)
    source = lane & 15
    for s in range(cols // 16):
        source = source + jnp.where((lane >> 4) == s, jump_table[s] * 16, 0)

    @pl.loop(0, cols // 16)
    def _(i):
        row = iota((16, cols), 0) + i * 16
        hot = row == jnp.concatenate([source, source], axis=0)
        jump_mat[pl.ds(pl.multiple_of(i * 16, 16), 16), :] = jnp.where(hot, 1.0, 0.0).astype(BF16)

    for copy in small[5:]:
        copy.wait()
    choices = fu.shape[0]
    band = iw.shape[1] // choices
    span = w2.shape[1]
    w2[...] = jnp.zeros(w2.shape, F32)
    for kb in range(groups):
        for j in range(choices):
            w2[(kb * choices + j) * GROUP : (kb * choices + j + 1) * GROUP, 0:band] = iw[
                kb * GROUP : (kb + 1) * GROUP, j * band : (j + 1) * band
            ]
    offset = band_start[0] - p * cap_rows + cap_rows // 2
    place_row = iota((span, span), 0)
    place_col = iota((span, span), 1)
    place = jnp.where((place_col == place_row + offset) & (place_row < band), 1.0, 0.0)
    w2p[...] = DISCOUNT * jnp.dot(
        w2[...], place, precision=lax.Precision.HIGHEST, preferred_element_type=F32
    )

    def landing_matrix(width, blocks):
        def columns(q):
            row = jnp.full(q.shape, -1000, jnp.int32)
            for q0, first, count in blocks:
                row = jnp.where(q >= q0, stacked_map(q - q0, first, count), row)
            return row

        parts = []
        for e0 in range(0, span, 32):
            e = iota((32, width), 0) + e0
            q = iota((32, width), 1)
            parts.append(lookup(cap_taps, columns(q) - e - 1))
        full = jnp.dot(
            w2p[...],
            jnp.concatenate(parts, axis=0),
            precision=lax.Precision.HIGHEST,
            preferred_element_type=F32,
        )
        high = rounded(full)
        q = iota(full.shape, 1)
        low_part = q < 0
        for q0, first, count in blocks:
            n = count * 3 * GROUP
            low_part = low_part | ((q >= q0 + 2 * n) & (q < q0 + 3 * n))
        return jnp.where(low_part, full - high, high)

    ext0 = 9 * GROUP * FIRST_PASS
    g_late[...] = landing_matrix(
        WIDE, tuple((i * BLOCK, EARLY + i, 1) for i in range(groups - EARLY))
    ).astype(BF16)
    g_second[...] = landing_matrix(WIDE, ((0, FIRST_PASS, EARLY - FIRST_PASS),)).astype(BF16)
    w2e = landing_matrix(WIDE, ((0, 0, FIRST_PASS),))
    elane = iota((GROUP, WIDE), 1)
    eye = jnp.where(iota((cap_rows, cap_rows), 0) == iota((cap_rows, cap_rows), 1), 1.0, 0.0)

    def turned(x):
        return lax.dot_general(
            eye,
            x,
            (((1,), (1,)), ((), ())),
            precision=lax.Precision.HIGHEST,
            preferred_element_type=F32,
        )

    flows = turned(fu[...])
    numbers = turned(ci[...].astype(F32))
    for kb in range(groups):
        for j0 in range(0, choices, 2):
            pair = []
            for j in (j0, j0 + 1):
                at = (kb * choices + j) * GROUP
                piece = w2e[at : at + GROUP, :]
                flow = flows[kb * GROUP : (kb + 1) * GROUP, j : j + 1]
                number = numbers[kb * GROUP : (kb + 1) * GROUP, j : j + 1]
                square = number * number
                f1 = rounded(flow)
                f2 = rounded(flow - f1)
                f3 = flow - f1 - f2
                q1 = rounded(square)
                q2 = square - q1
                for i, value in enumerate(
                    (f1, f2, f3, number, number, number, -q1, -q1, -q1, -q2, -q2, -q2)
                ):
                    piece = jnp.where(elane == ext0 + i, value, piece)
                pair.append(piece)
            at = (kb * choices + j0) * GROUP
            g_early[at : at + 2 * GROUP, :] = jnp.concatenate(pair, axis=0).astype(BF16)
    gain_row = gain[...].reshape(1, cols) * (1.0 / (LEVELS - 1))
    g1 = rounded(gain_row)
    g2 = rounded(gain_row - g1)
    g3 = gain_row - g1 - g2
    ext_count = WIDE - ext0
    erow = iota((ext_count, cols), 0)
    base = jnp.where(erow < 3, 1.0, 0.0)
    for i, value in enumerate((g1, g2, g3)):
        base = jnp.where(erow == 3 + i, value, base)
    ext_base[...] = base

    parts = temp_rows // GROUP

    def k_copy(g, ts, slot, to_next):
        src = xt.at[g, ts, GROUP : 2 * GROUP, :]
        side = 0 if to_next else 2
        return pltpu.make_async_remote_copy(
            src_ref=src,
            dst_ref=xt.at[g, ts, side * GROUP : (side + 1) * GROUP, :],
            send_sem=k_send.at[0 if to_next else 1, slot],
            recv_sem=k_recv.at[0 if to_next else 1, slot],
            device_id={"cap": p + 1 if to_next else p - 1},
            device_id_type=MESH,
        )

    def k_each(g, ts, slot, do, sending):
        @pl.when(has_next if sending else has_prev)
        def _():
            do(k_copy(g, ts, slot, True))

        @pl.when(has_prev if sending else has_next)
        def _():
            do(k_copy(g, ts, slot, False))

    every = pl.ds(0, temp_rows)

    def k_start(g):
        k_each(g, every, g, lambda c: c.start(), True)

    def k_wait_recv(g):
        k_each(g, every, g, lambda c: c.wait_recv(), False)

    def k_wait_send(g):
        k_each(g, every, g, lambda c: c.wait_send(), True)

    def part_rows(i):
        return pl.ds(pl.multiple_of(i * GROUP, GROUP), GROUP)

    def term(high_ref, low_ref, rows, x):
        high, low = halves(x)
        a = high_ref[rows, :]
        return mm(a, high) + mm(a, low) + mm(low_ref[rows, :], high)

    def own_term(g):
        x = v[pl.ds(g * GROUP, GROUP)].reshape(wide, cols)
        return term(a_mats.at[0], a_mats.at[1], slice(None), x)

    def mix(g, total, ts):
        high, low = halves(total)
        jumped = mm(high, jump_mat[...]) + mm(low, jump_mat[...])
        for i, t in enumerate(ts):
            rows = slice(i * GROUP, (i + 1) * GROUP)
            h = hazard[t]
            xt[g, t, GROUP : 2 * GROUP, :] = (1.0 - h) * total[rows] + h * jumped[rows]

    def first_part(i, own, lo, hi):
        rows = slice(lo * GROUP, hi * GROUP)
        return (
            own[rows]
            + term(a_tail.at[0], a_tail.at[1], rows, low_a[i].reshape(GROUP * FIRST, cols))
            + term(a_tail.at[2], a_tail.at[3], rows, high_a[i].reshape(GROUP * FIRST, cols))
        )

    def second_part(i, blocks):
        pad = jnp.zeros((a_final.shape[2] - 2 * GROUP * SECOND, cols), F32)
        x = jnp.concatenate([low_b[i], high_b[i], pad], axis=0)
        sums = []
        for lo, hi in blocks:
            sums.append(term(a_final.at[0], a_final.at[1], slice(lo * GROUP, hi * GROUP), x))
        return jnp.concatenate(sums, axis=0)

    def y_step(g):
        pad = jnp.zeros((wide - PACKED, cols), F32)
        total = own_term(g)
        y_wait_recv(g)
        for m, got in ((1, got_low), (2, got_high)):
            x = jnp.concatenate([got[g - 1], pad], axis=0)
            total = total + term(a_mats.at[2 * m], a_mats.at[2 * m + 1], slice(None), x)
        mix(g, total, range(temp_rows))

    def stacked(first_group, count, t):
        x = jnp.concatenate([xt[first_group + i, t] for i in range(count)], axis=0)
        high = rounded(x)
        return [high, x - high, high]

    def early(pair):
        sides = []
        for i in range(2):
            t = pair * 2 + i
            cost = jnp.full((ext_count, cols), temp_cost[t] * (1.0 / ((LEVELS - 1) * (LEVELS - 1))), F32)
            c1 = rounded(cost)
            c2 = rounded(cost - c1)
            c3 = cost - c1 - c2
            ext = ext_base[...]
            for r, value in enumerate((c1, c2, c3, c1, c2, c3)):
                ext = jnp.where(erow == 6 + r, value, ext)
            sides.append(jnp.concatenate(stacked(0, FIRST_PASS, t) + [ext], axis=0).astype(BF16))
        both = jnp.concatenate(sides, axis=1)
        for n in range(3):
            acc[pair, n] = mm(g_early[...], both[:, n * 256 : (n + 1) * 256])

    def second(pair):
        count = EARLY - FIRST_PASS
        pad = jnp.zeros((WIDE - 9 * GROUP * count, cols), F32)
        sides = []
        for i in range(2):
            rows = stacked(FIRST_PASS, count, pair * 2 + i) + [pad]
            sides.append(jnp.concatenate(rows, axis=0).astype(BF16))
        both = jnp.concatenate(sides, axis=1)
        for n in range(3):
            acc[pair, n] += mm(g_second[...], both[:, n * 256 : (n + 1) * 256])

    def build(g, pair):
        pad = jnp.zeros((BLOCK - 9 * GROUP, cols), F32)
        rows = slice((g - EARLY) * BLOCK, (g - EARLY + 1) * BLOCK)
        for i in range(2):
            rhs_late[pair, rows, i * cols : (i + 1) * cols] = jnp.concatenate(
                stacked(g, 1, pair * 2 + i) + [pad], axis=0
            ).astype(BF16)

    def late(pair, half, slot):
        pad = jnp.zeros((WIDE - (last - EARLY) * BLOCK - 9 * GROUP, cols), F32)
        final = jnp.concatenate(
            [
                jnp.concatenate(stacked(last, 1, pair * 2 + i) + [pad], axis=0).astype(BF16)
                for i in range(2)
            ],
            axis=1,
        )
        both = jnp.concatenate([rhs_late[pair], final], axis=0)
        for n in range(3):
            score = acc[pair, n] + mm(g_late[...], both[:, n * 256 : (n + 1) * 256])
            best = jnp.max(score.reshape(groups, choices, GROUP, 256), axis=1).reshape(cap_rows, 256)
            if n == 0:
                stage[half, slot, :, 0:256] = best
            elif n == 1:
                stage[half, slot, :, 256:384] = best[:, 0:128]
                stage[half, slot + 1, :, 0:128] = best[:, 128:256]
            else:
                stage[half, slot + 1, :, 128:384] = best

    pairs = temp_rows // 2

    def pair_loop(lo, hi, do):
        @pl.loop(lo, hi, step=2)
        def _(pair):
            do(pair)
            do(pair + 1)

    own = own_term(0)
    for part in range(2):
        y_each(part, lambda c: c.wait_send(), True, in_parts)
    y_start(2)
    for part in range(2):
        y_each(part, lambda c: c.wait_recv(), False, in_parts)
    everywhere = (0, temp_rows)
    mix(0, first_part(0, own, *everywhere) + second_part(0, (everywhere,)), range(temp_rows))
    k_start(0)

    def y_turn(g):
        y_wait_send(g)
        y_start(g + 2)
        y_step(g)
        k_start(g)

    @pl.loop(1, FIRST_PASS)
    def _(g):
        y_turn(g)
        pack(g + SLOTS)

    for done in range(FIRST_PASS):
        if done == FIRST_PASS - 1:
            y_turn(FIRST_PASS)
        k_wait_recv(done)
    pair_loop(0, pairs // 2, early)
    y_turn(EARLY - 1)
    pair_loop(pairs // 2, pairs, early)

    y_wait_send(EARLY)
    y_each(2, lambda c: c.start(), True, in_parts)
    y_step(EARLY)
    k_start(EARLY)
    for done in range(FIRST_PASS, EARLY):
        k_wait_recv(done)
    pair_loop(0, 8, second)
    y_wait_send(EARLY + 1)
    y_step(EARLY + 1)
    k_start(EARLY + 1)
    pair_loop(8, pairs, second)

    def k_part(i):
        k_each(last, part_rows(i), last + i, lambda c: c.start(), True)

    own = own_term(last)
    y_each(3, lambda c: c.start(), True, in_parts)
    y_each(2, lambda c: c.wait_recv(), False, in_parts)
    mix(last, first_part(1, own, 8, 24), range(8, 24))
    k_part(1)
    k_part(2)
    outer = jnp.concatenate([first_part(1, own, 24, 32), first_part(1, own, 0, 8)], axis=0)
    y_each(3, lambda c: c.wait_recv(), False, in_parts)
    mix(last, outer + second_part(1, ((24, 32), (0, 8))), (*range(24, 32), *range(8)))
    k_part(3)
    k_part(0)

    def build_both(pair):
        build(EARLY, pair)
        build(EARLY + 1, pair)

    k_wait_recv(EARLY)
    k_wait_recv(EARLY + 1)
    pair_loop(0, pairs, build_both)

    def octet(step):
        return lax.rem(step + 1, parts)

    def land(step):
        i = octet(step)
        k_each(last, part_rows(i), last + i, lambda c: c.wait_recv(), False)
        for slot in range(0, GROUP, 2):
            late(i * (GROUP // 2) + slot // 2, lax.rem(step, 2), slot)

    def turn(step):
        rows = part_rows(octet(step))
        half = lax.rem(step, 2)
        for kb in range(groups):
            at = slice(kb * GROUP, (kb + 1) * GROUP)
            out[at, rows, :] = jnp.swapaxes(stage[half, :, at, :], 0, 1)

    land(0)

    @pl.loop(1, parts)
    def _(step):
        land(step)
        turn(step - 1)

    turn(parts - 1)

    for part in range(2, 4):
        y_each(part, lambda c: c.wait_send(), True, in_parts)
    for g in range(last):
        k_wait_send(g)
    for i in range(parts):
        k_each(last, part_rows(i), last + i, lambda c: c.wait_send(), True)


def per_device(n_cap, n_temp, *args):
    value_next, interp_weights = args[0], args[6]
    cap_rows, temp_rows, cols = value_next.shape
    args = list(args)
    args[7], args[8] = args[7].T, args[8].T
    args[0] = pltpu.with_memory_space_constraint(value_next, pltpu.HBM)
    choices = args[8].shape[0]
    groups = cap_rows // GROUP
    rows = cap_rows * choices
    parts = temp_rows // GROUP
    hbm = pl.BlockSpec(memory_space=pl.ANY)
    result = pl.pallas_call(
        functools.partial(kernel, n_cap, n_temp),
        out_shape=pltpu.VMEM(value_next.shape, F32),
        in_specs=[hbm] * 5 + [pl.BlockSpec(memory_space=pltpu.SMEM)] + [hbm] * 5,
        out_specs=pl.BlockSpec(memory_space=pltpu.VMEM),
        scratch_shapes=[
            *(pltpu.SMEM(args[i].shape, args[i].dtype) for i in (1, 2, 3, 4)),
            pltpu.SMEM(args[10].shape, F32),
            pltpu.VMEM((cap_rows, temp_rows, cols), F32),
            pltpu.VMEM((SLOTS, PACKED, cols), F32),
            pltpu.VMEM((SLOTS, PACKED, cols), F32),
            pltpu.VMEM((groups - 2, PACKED, cols), F32),
            pltpu.VMEM((groups - 2, PACKED, cols), F32),
            pltpu.VMEM((2, GROUP, FIRST, cols), F32),
            pltpu.VMEM((2, GROUP, FIRST, cols), F32),
            *(pltpu.VMEM((2, GROUP * SECOND, cols), F32) for _ in range(4)),
            pltpu.VMEM((groups, temp_rows, 3 * GROUP, cols), F32),
            pltpu.VMEM((temp_rows // 2, 3, rows, 256), F32),
            pltpu.VMEM((2, GROUP, cap_rows, cols), F32),
            pltpu.VMEM(interp_weights.shape, F32),
            pltpu.VMEM((choices, cap_rows), jnp.int32),
            pltpu.VMEM((choices, cap_rows), F32),
            pltpu.VMEM((cols,), F32),
            pltpu.VMEM((6, GROUP * temp_rows, GROUP * temp_rows), BF16),
            pltpu.VMEM((4, GROUP * temp_rows, GROUP * FIRST), BF16),
            pltpu.VMEM((2, GROUP * temp_rows, 128), BF16),
            pltpu.VMEM((cols, cols), BF16),
            pltpu.VMEM((rows, 128), F32),
            pltpu.VMEM((rows, 128), F32),
            pltpu.VMEM((rows, WIDE), BF16),
            pltpu.VMEM((rows, WIDE), BF16),
            pltpu.VMEM((rows, WIDE), BF16),
            pltpu.VMEM((temp_rows // 2, (groups - 1 - EARLY) * BLOCK, 2 * cols), BF16),
            pltpu.VMEM((WIDE - 9 * GROUP * FIRST_PASS, cols), F32),
            pltpu.SemaphoreType.DMA((groups + 9,)),
            pltpu.SemaphoreType.DMA((2, groups + 2)),
            pltpu.SemaphoreType.DMA((2, groups + 2)),
            pltpu.SemaphoreType.DMA((2, groups - 1 + parts)),
            pltpu.SemaphoreType.DMA((2, groups - 1 + parts)),
        ],
        compiler_params=pltpu.CompilerParams(
            collective_id=0, has_side_effects=True, vmem_limit_bytes=58 * 1024 * 1024
        ),
        cost_estimate=pl.CostEstimate(flops=6_000_000_000, bytes_accessed=8_000_000, transcendentals=0),
    )(*args)
    pieces = 8
    return pl.pallas_call(
        functools.partial(leave, pieces),
        out_shape=jax.ShapeDtypeStruct(value_next.shape, F32),
        in_specs=[pl.BlockSpec(memory_space=pltpu.VMEM)],
        out_specs=hbm,
        scratch_shapes=[pltpu.SemaphoreType.DMA((pieces,))],
        compiler_params=pltpu.CompilerParams(vmem_limit_bytes=4 * 1024 * 1024),
    )(pltpu.with_memory_space_constraint(result, pltpu.VMEM))


def leave(pieces, src, dst, sem):
    rows = src.shape[0] // pieces
    copies = [
        pltpu.make_async_copy(
            src.at[pl.ds(i * rows, rows)], dst.at[pl.ds(i * rows, rows)], sem.at[i]
        )
        for i in range(pieces)
    ]
    for copy in copies:
        copy.start()
    for copy in copies:
        copy.wait()


def solution(mesh):
    in_specs = (
        P("cap", "temp", None),
        P(),
        P(),
        P("temp"),
        P(),
        P("cap"),
        P("cap", None),
        P("cap", None),
        P("cap", None),
        P(),
        P("temp"),
    )
    return jax.shard_map(
        functools.partial(per_device, mesh.shape["cap"], mesh.shape["temp"]),
        mesh=mesh,
        in_specs=in_specs,
        out_specs=P("cap", "temp", None),
        check_vma=False,
    )
```

```python
import functools

import jax
import jax.numpy as jnp
from jax import lax
from jax.experimental import pallas as pl
from jax.experimental.pallas import tpu as pltpu
from jax.sharding import PartitionSpec as P

RADIUS = 31
TAPS = 63
LEVELS = 21
DISCOUNT = 0.96
GROUP = 8
PACKED = GROUP * RADIUS
FIRST = 24
SECOND = RADIUS - FIRST
SLOTS = 4
EARLY = 5
FIRST_PASS = 3
BLOCK = 80
WIDE = 256
MESH = pl.DeviceIdType.MESH
F32 = jnp.float32
BF16 = jnp.bfloat16


def iota(shape, axis):
    return lax.broadcasted_iota(jnp.int32, shape, axis)


def rounded(x):
    return x.astype(BF16).astype(F32)


def halves(x):
    high = x.astype(BF16)
    return high, (x - high.astype(F32)).astype(BF16)


def mm(a, b):
    return jnp.dot(a, b, preferred_element_type=F32)


def count_steps(x, step, most):
    total = jnp.zeros_like(x)
    for i in range(1, most + 1):
        total = total + jnp.where(x >= step * i, 1, 0)
    return total


def lookup(taps_ref, index):
    found = jnp.zeros(index.shape, F32)
    for d in range(TAPS):
        found = jnp.where(index == d, taps_ref[d], found)
    return found


def stacked_map(q, first_group, groups):
    n = groups * 3 * GROUP
    w = q - n * count_steps(q, n, 2)
    g = count_steps(w, 3 * GROUP, groups - 1)
    u = w - 3 * GROUP * g
    side = count_steps(u, GROUP, 2)
    row = side * 64 + (g + first_group) * GROUP + (u - GROUP * side)
    return jnp.where(q < 3 * n, row, -1000)


def kernel(
    n_cap,
    n_temp,
    v_hbm,
    cap_taps_hbm,
    temp_taps_hbm,
    hazard_hbm,
    jump_table_hbm,
    band_start,
    iw_hbm,
    ci_hbm,
    fu_hbm,
    gain_hbm,
    temp_cost_hbm,
    out,
    cap_taps,
    temp_taps,
    hazard,
    jump_table,
    temp_cost,
    v,
    send_up,
    send_down,
    got_low,
    got_high,
    low_a,
    high_a,
    low_b,
    high_b,
    up_b,
    down_b,
    xt,
    acc,
    stage,
    iw,
    ci,
    fu,
    gain,
    a_mats,
    a_tail,
    a_final,
    jump_mat,
    w2,
    w2p,
    g_early,
    g_second,
    g_late,
    rhs_late,
    ext_base,
    local_sem,
    y_send,
    y_recv,
    k_sent,
    k_recv,
):
    p = lax.axis_index("cap")
    b = lax.axis_index("temp")
    cap_rows, temp_rows, cols = v.shape
    groups = cap_rows // GROUP
    last = groups - 1
    has_low, has_high = b > 0, b < n_temp - 1
    has_prev, has_next = p > 0, p < n_cap - 1

    def load(g):
        rows = pl.ds(g * GROUP, GROUP)
        return pltpu.make_async_copy(v_hbm.at[rows], v.at[rows], local_sem.at[g])

    small = [
        pltpu.make_async_copy(src, dst, local_sem.at[groups + i])
        for i, (src, dst) in enumerate(
            (
                (temp_taps_hbm, temp_taps),
                (hazard_hbm, hazard),
                (jump_table_hbm, jump_table),
                (cap_taps_hbm, cap_taps),
                (temp_cost_hbm, temp_cost),
                (iw_hbm, iw),
                (ci_hbm, ci),
                (fu_hbm, fu),
                (gain_hbm, gain),
            )
        )
    ]
    barrier = pltpu.get_barrier_semaphore()
    for there, axis, at in (
        (has_low, "temp", b - 1),
        (has_high, "temp", b + 1),
        (has_prev, "cap", p - 1),
        (has_next, "cap", p + 1),
    ):

        @pl.when(there)
        def _(axis=axis, at=at):
            pl.semaphore_signal(barrier, inc=1, device_id={axis: at}, device_id_type=MESH)

    for g in range(groups):
        load(g).start()
    for copy in small:
        copy.start()

    def going(way, src, dst, slot):
        return pltpu.make_async_remote_copy(
            src_ref=src,
            dst_ref=dst,
            send_sem=y_send.at[way, slot],
            recv_sem=y_recv.at[way, slot],
            device_id={"temp": b + 1 - 2 * way},
            device_id_type=MESH,
        )

    def up(g):
        return going(0, send_up.at[lax.rem(g, SLOTS)], got_low.at[g - 1], g)

    def down(g):
        return going(1, send_down.at[lax.rem(g, SLOTS)], got_high.at[g - 1], g)

    def part_source(part, first):
        if part % 2:
            return None
        source = v_hbm.at[pl.ds(0, GROUP)] if part == 0 else v.at[pl.ds(last * GROUP, GROUP)]
        return source.at[:, pl.ds(first, FIRST), :]

    part_slots = (0, groups, last, groups + 1)

    def up_part(part):
        i = part // 2
        if part % 2 == 0:
            return going(0, part_source(part, SECOND + 1), low_a.at[i], part_slots[part])
        return going(0, up_b.at[i], low_b.at[i], part_slots[part])

    def down_part(part):
        i = part // 2
        if part % 2 == 0:
            return going(1, part_source(part, 0), high_a.at[i], part_slots[part])
        return going(1, down_b.at[i], high_b.at[i], part_slots[part])

    def pack(g):
        load(g).wait()
        slot = lax.rem(g, SLOTS)
        for k in range(GROUP):
            rows = slice(RADIUS * k, RADIUS * (k + 1))
            send_up[slot, rows, :] = v[g * GROUP + k, 1 : RADIUS + 1, :]
            send_down[slot, rows, :] = v[g * GROUP + k, 0:RADIUS, :]

    def y_each(g, do, sending, ways=(up, down)):
        @pl.when(has_high if sending else has_low)
        def _():
            do(ways[0](g))

        @pl.when(has_low if sending else has_high)
        def _():
            do(ways[1](g))

    in_parts = (up_part, down_part)

    def pack_second(i):
        g = i * last
        load(g).wait()
        for k in range(GROUP):
            rows = slice(SECOND * k, SECOND * (k + 1))
            up_b[i, rows, :] = v[g * GROUP + k, 1 : SECOND + 1, :]
            down_b[i, rows, :] = v[g * GROUP + k, FIRST : FIRST + SECOND, :]

    def y_start(g):
        y_each(g, lambda c: c.start(), True)

    def y_wait_send(g):
        y_each(g, lambda c: c.wait_send(), True)

    def y_wait_recv(g):
        y_each(g, lambda c: c.wait_recv(), False)

    neighbours = sum(jnp.where(there, 1, 0) for there in (has_low, has_high, has_prev, has_next))
    pl.semaphore_wait(barrier, neighbours)
    y_each(0, lambda c: c.start(), True, in_parts)
    pack_second(0)
    y_each(1, lambda c: c.start(), True, in_parts)
    pack(1)
    y_start(1)
    for g in range(2, SLOTS + 1):
        pack(g)
    pack_second(1)
    for copy in small[:5]:
        copy.wait()

    @pl.when(jnp.logical_not(has_low))
    def _():
        @pl.loop(0, last - 1)
        def _(g):
            got_low[g] = jnp.zeros((PACKED, cols), F32)

        low_a[...] = jnp.zeros(low_a.shape, F32)
        low_b[...] = jnp.zeros(low_b.shape, F32)

    @pl.when(jnp.logical_not(has_high))
    def _():
        @pl.loop(0, last - 1)
        def _(g):
            got_high[g] = jnp.zeros((PACKED, cols), F32)

        high_a[...] = jnp.zeros(high_a.shape, F32)
        high_b[...] = jnp.zeros(high_b.shape, F32)

    for there, side in ((has_prev, 0), (has_next, 2)):

        @pl.when(jnp.logical_not(there))
        def _(side=side):
            @pl.loop(0, groups)
            def _(g):
                @pl.loop(0, temp_rows)
                def _(t):
                    xt[g, t, side * GROUP : (side + 1) * GROUP, :] = jnp.zeros((GROUP, cols), F32)

    wide = GROUP * temp_rows

    def temperature(high_ref, low_ref, width, blocks):
        t_of = iota((temp_rows, width), 0)
        col = iota((temp_rows, width), 1)
        col8 = iota((GROUP, width), 1)
        index = jnp.full(col.shape, -1, jnp.int32)
        k_of = jnp.full(col8.shape, -1, jnp.int32)
        for q0, per, tap in blocks:
            k = count_steps(col - q0, per, GROUP - 1)
            here = (col >= q0) & (col < q0 + GROUP * per)
            index = jnp.where(here, col - q0 - per * k + tap - t_of, index)
            here = (col8 >= q0) & (col8 < q0 + GROUP * per)
            k_of = jnp.where(here, count_steps(col8 - q0, per, GROUP - 1), k_of)
        found = lookup(temp_taps, index)
        same = k_of == iota((GROUP, width), 0)
        for t in range(0, temp_rows, 2):
            block = jnp.concatenate(
                [jnp.where(same, found[t + i : t + i + 1, :], 0.0) for i in range(2)], axis=0
            )
            high, low = halves(block)
            high_ref[t * GROUP : (t + 2) * GROUP, :] = high
            low_ref[t * GROUP : (t + 2) * GROUP, :] = low

    for m, per, tap in ((0, temp_rows, RADIUS), (1, RADIUS, 0), (2, RADIUS, TAPS)):
        temperature(a_mats.at[2 * m], a_mats.at[2 * m + 1], wide, ((0, per, tap),))
    for m, tap in ((0, SECOND), (1, TAPS)):
        temperature(a_tail.at[2 * m], a_tail.at[2 * m + 1], GROUP * FIRST, ((0, FIRST, tap),))
    temperature(
        a_final.at[0],
        a_final.at[1],
        a_final.shape[2],
        ((0, SECOND, 0), (GROUP * SECOND, SECOND, TAPS + FIRST)),
    )

    lane = iota((GROUP, cols), 1)
    source = lane & 15
    for s in range(cols // 16):
        source = source + jnp.where((lane >> 4) == s, jump_table[s] * 16, 0)

    @pl.loop(0, cols // 16)
    def _(i):
        row = iota((16, cols), 0) + i * 16
        hot = row == jnp.concatenate([source, source], axis=0)
        jump_mat[pl.ds(pl.multiple_of(i * 16, 16), 16), :] = jnp.where(hot, 1.0, 0.0).astype(BF16)

    for copy in small[5:]:
        copy.wait()
    choices = fu.shape[0]
    band = iw.shape[1] // choices
    span = w2.shape[1]
    w2[...] = jnp.zeros(w2.shape, F32)
    for kb in range(groups):
        for j in range(choices):
            w2[(kb * choices + j) * GROUP : (kb * choices + j + 1) * GROUP, 0:band] = iw[
                kb * GROUP : (kb + 1) * GROUP, j * band : (j + 1) * band
            ]
    offset = band_start[0] - p * cap_rows + cap_rows // 2
    place_row = iota((span, span), 0)
    place_col = iota((span, span), 1)
    place = jnp.where((place_col == place_row + offset) & (place_row < band), 1.0, 0.0)
    w2p[...] = DISCOUNT * jnp.dot(
        w2[...], place, precision=lax.Precision.HIGHEST, preferred_element_type=F32
    )

    def landing_matrix(width, blocks):
        def columns(q):
            row = jnp.full(q.shape, -1000, jnp.int32)
            for q0, first, count in blocks:
                row = jnp.where(q >= q0, stacked_map(q - q0, first, count), row)
            return row

        parts = []
        for e0 in range(0, span, 32):
            e = iota((32, width), 0) + e0
            q = iota((32, width), 1)
            parts.append(lookup(cap_taps, columns(q) - e - 1))
        full = jnp.dot(
            w2p[...],
            jnp.concatenate(parts, axis=0),
            precision=lax.Precision.HIGHEST,
            preferred_element_type=F32,
        )
        high = rounded(full)
        q = iota(full.shape, 1)
        low_part = q < 0
        for q0, first, count in blocks:
            n = count * 3 * GROUP
            low_part = low_part | ((q >= q0 + 2 * n) & (q < q0 + 3 * n))
        return jnp.where(low_part, full - high, high)

    ext0 = 9 * GROUP * FIRST_PASS
    g_late[...] = landing_matrix(
        WIDE, tuple((i * BLOCK, EARLY + i, 1) for i in range(groups - EARLY))
    ).astype(BF16)
    g_second[...] = landing_matrix(WIDE, ((0, FIRST_PASS, EARLY - FIRST_PASS),)).astype(BF16)
    w2e = landing_matrix(WIDE, ((0, 0, FIRST_PASS),))
    elane = iota((GROUP, WIDE), 1)
    eye = jnp.where(iota((cap_rows, cap_rows), 0) == iota((cap_rows, cap_rows), 1), 1.0, 0.0)

    def turned(x):
        return lax.dot_general(
            eye,
            x,
            (((1,), (1,)), ((), ())),
            precision=lax.Precision.HIGHEST,
            preferred_element_type=F32,
        )

    flows = turned(fu[...])
    numbers = turned(ci[...].astype(F32))
    for kb in range(groups):
        for j0 in range(0, choices, 2):
            pair = []
            for j in (j0, j0 + 1):
                at = (kb * choices + j) * GROUP
                piece = w2e[at : at + GROUP, :]
                flow = flows[kb * GROUP : (kb + 1) * GROUP, j : j + 1]
                number = numbers[kb * GROUP : (kb + 1) * GROUP, j : j + 1]
                square = number * number
                f1 = rounded(flow)
                f2 = rounded(flow - f1)
                f3 = flow - f1 - f2
                q1 = rounded(square)
                q2 = square - q1
                for i, value in enumerate(
                    (f1, f2, f3, number, number, number, -q1, -q1, -q1, -q2, -q2, -q2)
                ):
                    piece = jnp.where(elane == ext0 + i, value, piece)
                pair.append(piece)
            at = (kb * choices + j0) * GROUP
            g_early[at : at + 2 * GROUP, :] = jnp.concatenate(pair, axis=0).astype(BF16)
    gain_row = gain[...].reshape(1, cols) * (1.0 / (LEVELS - 1))
    g1 = rounded(gain_row)
    g2 = rounded(gain_row - g1)
    g3 = gain_row - g1 - g2
    ext_count = WIDE - ext0
    erow = iota((ext_count, cols), 0)
    base = jnp.where(erow < 3, 1.0, 0.0)
    for i, value in enumerate((g1, g2, g3)):
        base = jnp.where(erow == 3 + i, value, base)
    ext_base[...] = base

    parts = temp_rows // GROUP

    def k_copy(g, ts, slot, to_next):
        src = xt.at[g, ts, GROUP : 2 * GROUP, :]
        side = 0 if to_next else 2
        return pltpu.make_async_remote_copy(
            src_ref=src,
            dst_ref=xt.at[g, ts, side * GROUP : (side + 1) * GROUP, :],
            send_sem=k_sent.at[0 if to_next else 1, slot],
            recv_sem=k_recv.at[0 if to_next else 1, slot],
            device_id={"cap": p + 1 if to_next else p - 1},
            device_id_type=MESH,
        )

    def k_each(g, ts, slot, do, sending):
        @pl.when(has_next if sending else has_prev)
        def _():
            do(k_copy(g, ts, slot, True))

        @pl.when(has_prev if sending else has_next)
        def _():
            do(k_copy(g, ts, slot, False))

    odd = lax.rem(p, 2) == 1
    even = lax.rem(p, 2) == 0

    def k_send(g, ts, slot):
        for there, to_next in (
            (odd & has_next, True),
            (even & has_prev, False),
            (even & has_next, True),
            (odd & has_prev, False),
        ):

            @pl.when(there)
            def _(to_next=to_next):
                k_copy(g, ts, slot, to_next).start()

    every = pl.ds(0, temp_rows)

    def k_start(g):
        k_send(g, every, g)

    def k_wait_recv(g):
        k_each(g, every, g, lambda c: c.wait_recv(), False)

    def k_wait_send(g):
        k_each(g, every, g, lambda c: c.wait_send(), True)

    def part_rows(i):
        return pl.ds(pl.multiple_of(i * GROUP, GROUP), GROUP)

    def term(high_ref, low_ref, rows, x):
        high, low = halves(x)
        a = high_ref[rows, :]
        return mm(a, high) + mm(a, low) + mm(low_ref[rows, :], high)

    def own_term(g):
        x = v[pl.ds(g * GROUP, GROUP)].reshape(wide, cols)
        return term(a_mats.at[0], a_mats.at[1], slice(None), x)

    def mix(g, total, ts):
        high, low = halves(total)
        jumped = mm(high, jump_mat[...]) + mm(low, jump_mat[...])
        for i, t in enumerate(ts):
            rows = slice(i * GROUP, (i + 1) * GROUP)
            h = hazard[t]
            xt[g, t, GROUP : 2 * GROUP, :] = (1.0 - h) * total[rows] + h * jumped[rows]

    def first_part(i, own, lo, hi):
        rows = slice(lo * GROUP, hi * GROUP)
        return (
            own[rows]
            + term(a_tail.at[0], a_tail.at[1], rows, low_a[i].reshape(GROUP * FIRST, cols))
            + term(a_tail.at[2], a_tail.at[3], rows, high_a[i].reshape(GROUP * FIRST, cols))
        )

    def second_part(i, blocks):
        pad = jnp.zeros((a_final.shape[2] - 2 * GROUP * SECOND, cols), F32)
        x = jnp.concatenate([low_b[i], high_b[i], pad], axis=0)
        sums = []
        for lo, hi in blocks:
            sums.append(term(a_final.at[0], a_final.at[1], slice(lo * GROUP, hi * GROUP), x))
        return jnp.concatenate(sums, axis=0)

    def y_step(g):
        pad = jnp.zeros((wide - PACKED, cols), F32)
        total = own_term(g)
        y_wait_recv(g)
        for m, got in ((1, got_low), (2, got_high)):
            x = jnp.concatenate([got[g - 1], pad], axis=0)
            total = total + term(a_mats.at[2 * m], a_mats.at[2 * m + 1], slice(None), x)
        mix(g, total, range(temp_rows))

    def stacked(first_group, count, t):
        x = jnp.concatenate([xt[first_group + i, t] for i in range(count)], axis=0)
        high = rounded(x)
        return [high, x - high, high]

    def early(pair):
        sides = []
        for i in range(2):
            t = pair * 2 + i
            cost = jnp.full((ext_count, cols), temp_cost[t] * (1.0 / ((LEVELS - 1) * (LEVELS - 1))), F32)
            c1 = rounded(cost)
            c2 = rounded(cost - c1)
            c3 = cost - c1 - c2
            ext = ext_base[...]
            for r, value in enumerate((c1, c2, c3, c1, c2, c3)):
                ext = jnp.where(erow == 6 + r, value, ext)
            sides.append(jnp.concatenate(stacked(0, FIRST_PASS, t) + [ext], axis=0).astype(BF16))
        both = jnp.concatenate(sides, axis=1)
        for n in range(3):
            acc[pair, n] = mm(g_early[...], both[:, n * 256 : (n + 1) * 256])

    def second(pair):
        count = EARLY - FIRST_PASS
        pad = jnp.zeros((WIDE - 9 * GROUP * count, cols), F32)
        sides = []
        for i in range(2):
            rows = stacked(FIRST_PASS, count, pair * 2 + i) + [pad]
            sides.append(jnp.concatenate(rows, axis=0).astype(BF16))
        both = jnp.concatenate(sides, axis=1)
        for n in range(3):
            acc[pair, n] += mm(g_second[...], both[:, n * 256 : (n + 1) * 256])

    def build(g, pair):
        pad = jnp.zeros((BLOCK - 9 * GROUP, cols), F32)
        rows = slice((g - EARLY) * BLOCK, (g - EARLY + 1) * BLOCK)
        for i in range(2):
            rhs_late[pair, rows, i * cols : (i + 1) * cols] = jnp.concatenate(
                stacked(g, 1, pair * 2 + i) + [pad], axis=0
            ).astype(BF16)

    def late(pair, half, slot):
        pad = jnp.zeros((WIDE - (last - EARLY) * BLOCK - 9 * GROUP, cols), F32)
        final = jnp.concatenate(
            [
                jnp.concatenate(stacked(last, 1, pair * 2 + i) + [pad], axis=0).astype(BF16)
                for i in range(2)
            ],
            axis=1,
        )
        both = jnp.concatenate([rhs_late[pair], final], axis=0)
        for n in range(3):
            score = acc[pair, n] + mm(g_late[...], both[:, n * 256 : (n + 1) * 256])
            best = jnp.max(score.reshape(groups, choices, GROUP, 256), axis=1).reshape(cap_rows, 256)
            if n == 0:
                stage[half, slot, :, 0:256] = best
            elif n == 1:
                stage[half, slot, :, 256:384] = best[:, 0:128]
                stage[half, slot + 1, :, 0:128] = best[:, 128:256]
            else:
                stage[half, slot + 1, :, 128:384] = best

    pairs = temp_rows // 2

    def pair_loop(lo, hi, do):
        @pl.loop(lo, hi, step=2)
        def _(pair):
            do(pair)
            do(pair + 1)

    own = own_term(0)
    for part in range(2):
        y_each(part, lambda c: c.wait_send(), True, in_parts)
    y_start(2)
    for part in range(2):
        y_each(part, lambda c: c.wait_recv(), False, in_parts)
    everywhere = (0, temp_rows)
    mix(0, first_part(0, own, *everywhere) + second_part(0, (everywhere,)), range(temp_rows))
    k_start(0)

    def y_turn(g):
        y_wait_send(g)
        y_start(g + 2)
        y_step(g)
        k_start(g)

    @pl.loop(1, FIRST_PASS)
    def _(g):
        y_turn(g)
        pack(g + SLOTS)

    for done in range(FIRST_PASS):
        if done == FIRST_PASS - 1:
            y_turn(FIRST_PASS)
        k_wait_recv(done)
    pair_loop(0, pairs // 2, early)
    y_turn(EARLY - 1)
    pair_loop(pairs // 2, pairs, early)

    y_wait_send(EARLY)
    y_each(2, lambda c: c.start(), True, in_parts)
    y_step(EARLY)
    k_start(EARLY)
    for done in range(FIRST_PASS, EARLY):
        k_wait_recv(done)
    pair_loop(0, 8, second)
    y_wait_send(EARLY + 1)
    y_step(EARLY + 1)
    k_start(EARLY + 1)
    pair_loop(8, 12, second)
    y_each(3, lambda c: c.start(), True, in_parts)
    pair_loop(12, pairs, second)

    def k_part(i):
        k_send(last, part_rows(i), last + i)

    own = own_term(last)
    y_each(2, lambda c: c.wait_recv(), False, in_parts)
    mix(last, first_part(1, own, 8, 24), range(8, 24))
    k_part(1)
    k_part(2)
    outer = jnp.concatenate([first_part(1, own, 24, 32), first_part(1, own, 0, 8)], axis=0)
    y_each(3, lambda c: c.wait_recv(), False, in_parts)
    mix(last, outer + second_part(1, ((24, 32), (0, 8))), (*range(24, 32), *range(8)))
    k_part(3)
    k_part(0)

    def build_both(pair):
        build(EARLY, pair)
        build(EARLY + 1, pair)

    k_wait_recv(EARLY)
    k_wait_recv(EARLY + 1)
    pair_loop(0, pairs, build_both)

    def octet(step):
        return lax.rem(step + 1, parts)

    def land(step):
        i = octet(step)
        k_each(last, part_rows(i), last + i, lambda c: c.wait_recv(), False)
        for slot in range(0, GROUP, 2):
            late(i * (GROUP // 2) + slot // 2, lax.rem(step, 2), slot)

    def turn(step):
        rows = part_rows(octet(step))
        half = lax.rem(step, 2)
        for kb in range(groups):
            at = slice(kb * GROUP, (kb + 1) * GROUP)
            out[at, rows, :] = jnp.swapaxes(stage[half, :, at, :], 0, 1)

    land(0)

    @pl.loop(1, parts)
    def _(step):
        land(step)
        turn(step - 1)

    turn(parts - 1)

    for part in range(2, 4):
        y_each(part, lambda c: c.wait_send(), True, in_parts)
    for g in range(last):
        k_wait_send(g)
    for i in range(parts):
        k_each(last, part_rows(i), last + i, lambda c: c.wait_send(), True)


def per_device(n_cap, n_temp, *args):
    value_next, interp_weights = args[0], args[6]
    cap_rows, temp_rows, cols = value_next.shape
    args = list(args)
    args[7], args[8] = args[7].T, args[8].T
    args[0] = pltpu.with_memory_space_constraint(value_next, pltpu.HBM)
    choices = args[8].shape[0]
    groups = cap_rows // GROUP
    rows = cap_rows * choices
    parts = temp_rows // GROUP
    hbm = pl.BlockSpec(memory_space=pl.ANY)
    return pl.pallas_call(
        functools.partial(kernel, n_cap, n_temp),
        out_shape=pltpu.VMEM(value_next.shape, F32),
        in_specs=[hbm] * 5 + [pl.BlockSpec(memory_space=pltpu.SMEM)] + [hbm] * 5,
        out_specs=pl.BlockSpec(memory_space=pltpu.VMEM),
        scratch_shapes=[
            *(pltpu.SMEM(args[i].shape, args[i].dtype) for i in (1, 2, 3, 4)),
            pltpu.SMEM(args[10].shape, F32),
            pltpu.VMEM((cap_rows, temp_rows, cols), F32),
            pltpu.VMEM((SLOTS, PACKED, cols), F32),
            pltpu.VMEM((SLOTS, PACKED, cols), F32),
            pltpu.VMEM((groups - 2, PACKED, cols), F32),
            pltpu.VMEM((groups - 2, PACKED, cols), F32),
            pltpu.VMEM((2, GROUP, FIRST, cols), F32),
            pltpu.VMEM((2, GROUP, FIRST, cols), F32),
            *(pltpu.VMEM((2, GROUP * SECOND, cols), F32) for _ in range(4)),
            pltpu.VMEM((groups, temp_rows, 3 * GROUP, cols), F32),
            pltpu.VMEM((temp_rows // 2, 3, rows, 256), F32),
            pltpu.VMEM((2, GROUP, cap_rows, cols), F32),
            pltpu.VMEM(interp_weights.shape, F32),
            pltpu.VMEM((choices, cap_rows), jnp.int32),
            pltpu.VMEM((choices, cap_rows), F32),
            pltpu.VMEM((cols,), F32),
            pltpu.VMEM((6, GROUP * temp_rows, GROUP * temp_rows), BF16),
            pltpu.VMEM((4, GROUP * temp_rows, GROUP * FIRST), BF16),
            pltpu.VMEM((2, GROUP * temp_rows, 128), BF16),
            pltpu.VMEM((cols, cols), BF16),
            pltpu.VMEM((rows, 128), F32),
            pltpu.VMEM((rows, 128), F32),
            pltpu.VMEM((rows, WIDE), BF16),
            pltpu.VMEM((rows, WIDE), BF16),
            pltpu.VMEM((rows, WIDE), BF16),
            pltpu.VMEM((temp_rows // 2, (groups - 1 - EARLY) * BLOCK, 2 * cols), BF16),
            pltpu.VMEM((WIDE - 9 * GROUP * FIRST_PASS, cols), F32),
            pltpu.SemaphoreType.DMA((groups + 9,)),
            pltpu.SemaphoreType.DMA((2, groups + 2)),
            pltpu.SemaphoreType.DMA((2, groups + 2)),
            pltpu.SemaphoreType.DMA((2, groups - 1 + parts)),
            pltpu.SemaphoreType.DMA((2, groups - 1 + parts)),
        ],
        compiler_params=pltpu.CompilerParams(
            collective_id=0, has_side_effects=True, vmem_limit_bytes=58 * 1024 * 1024
        ),
        cost_estimate=pl.CostEstimate(flops=6_000_000_000, bytes_accessed=8_000_000, transcendentals=0),
    )(*args)


def solution(mesh):
    in_specs = (
        P("cap", "temp", None),
        P(),
        P(),
        P("temp"),
        P(),
        P("cap"),
        P("cap", None),
        P("cap", None),
        P("cap", None),
        P(),
        P("temp"),
    )
    return jax.shard_map(
        functools.partial(per_device, mesh.shape["cap"], mesh.shape["temp"]),
        mesh=mesh,
        in_specs=in_specs,
        out_specs=P("cap", "temp", None),
        check_vma=False,
    )
```

```python
import functools

import jax
import jax.numpy as jnp
from jax import lax
from jax.experimental import pallas as pl
from jax.experimental.pallas import tpu as pltpu
from jax.sharding import PartitionSpec as P

RADIUS = 31
TAPS = 63
LEVELS = 21
DISCOUNT = 0.96
GROUP = 8
PACKED = GROUP * RADIUS
FIRST = 24
SECOND = RADIUS - FIRST
SLOTS = 4
EARLY = 5
FIRST_PASS = 3
BLOCK = 80
WIDE = 256
MESH = pl.DeviceIdType.MESH
F32 = jnp.float32
BF16 = jnp.bfloat16


def iota(shape, axis):
    return lax.broadcasted_iota(jnp.int32, shape, axis)


def rounded(x):
    return x.astype(BF16).astype(F32)


def halves(x):
    high = x.astype(BF16)
    return high, (x - high.astype(F32)).astype(BF16)


def mm(a, b):
    return jnp.dot(a, b, preferred_element_type=F32)


def count_steps(x, step, most):
    total = jnp.zeros_like(x)
    for i in range(1, most + 1):
        total = total + jnp.where(x >= step * i, 1, 0)
    return total


def lookup(taps_ref, index):
    found = jnp.zeros(index.shape, F32)
    for d in range(TAPS):
        found = jnp.where(index == d, taps_ref[d], found)
    return found


def stacked_map(q, first_group, groups):
    n = groups * 3 * GROUP
    w = q - n * count_steps(q, n, 2)
    g = count_steps(w, 3 * GROUP, groups - 1)
    u = w - 3 * GROUP * g
    side = count_steps(u, GROUP, 2)
    row = side * 64 + (g + first_group) * GROUP + (u - GROUP * side)
    return jnp.where(q < 3 * n, row, -1000)


def kernel(
    n_cap,
    n_temp,
    v_hbm,
    cap_taps_hbm,
    temp_taps_hbm,
    hazard_hbm,
    jump_table_hbm,
    band_start,
    iw_hbm,
    ci_hbm,
    fu_hbm,
    gain_hbm,
    temp_cost_hbm,
    out,
    cap_taps,
    temp_taps,
    hazard,
    jump_table,
    temp_cost,
    v,
    send_up,
    send_down,
    got_low,
    got_high,
    low_a,
    high_a,
    low_b,
    high_b,
    up_b,
    down_b,
    xt,
    acc,
    stage,
    iw,
    ci,
    fu,
    gain,
    a_mats,
    a_tail,
    a_final,
    jump_mat,
    w2,
    w2p,
    g_early,
    g_second,
    g_late,
    rhs_late,
    ext_base,
    local_sem,
    y_send,
    y_recv,
    k_sent,
    k_recv,
):
    p = lax.axis_index("cap")
    b = lax.axis_index("temp")
    cap_rows, temp_rows, cols = v.shape
    groups = cap_rows // GROUP
    last = groups - 1
    has_low, has_high = b > 0, b < n_temp - 1
    has_prev, has_next = p > 0, p < n_cap - 1

    def load(g):
        rows = pl.ds(g * GROUP, GROUP)
        return pltpu.make_async_copy(v_hbm.at[rows], v.at[rows], local_sem.at[g])

    small = [
        pltpu.make_async_copy(src, dst, local_sem.at[groups + i])
        for i, (src, dst) in enumerate(
            (
                (temp_taps_hbm, temp_taps),
                (hazard_hbm, hazard),
                (jump_table_hbm, jump_table),
                (cap_taps_hbm, cap_taps),
                (temp_cost_hbm, temp_cost),
                (iw_hbm, iw),
                (ci_hbm, ci),
                (fu_hbm, fu),
                (gain_hbm, gain),
            )
        )
    ]
    barrier = pltpu.get_barrier_semaphore()
    for there, axis, at in (
        (has_low, "temp", b - 1),
        (has_high, "temp", b + 1),
        (has_prev, "cap", p - 1),
        (has_next, "cap", p + 1),
    ):

        @pl.when(there)
        def _(axis=axis, at=at):
            pl.semaphore_signal(barrier, inc=1, device_id={axis: at}, device_id_type=MESH)

    for g in range(groups):
        load(g).start()
    for copy in small:
        copy.start()

    def going(way, src, dst, slot):
        return pltpu.make_async_remote_copy(
            src_ref=src,
            dst_ref=dst,
            send_sem=y_send.at[way, slot],
            recv_sem=y_recv.at[way, slot],
            device_id={"temp": b + 1 - 2 * way},
            device_id_type=MESH,
        )

    def up(g):
        return going(0, send_up.at[lax.rem(g, SLOTS)], got_low.at[g - 1], g)

    def down(g):
        return going(1, send_down.at[lax.rem(g, SLOTS)], got_high.at[g - 1], g)

    def part_source(part, first):
        if part % 2:
            return None
        source = v_hbm.at[pl.ds(0, GROUP)] if part == 0 else v.at[pl.ds(last * GROUP, GROUP)]
        return source.at[:, pl.ds(first, FIRST), :]

    part_slots = (0, groups, last, groups + 1)

    def up_part(part):
        i = part // 2
        if part % 2 == 0:
            return going(0, part_source(part, SECOND + 1), low_a.at[i], part_slots[part])
        return going(0, up_b.at[i], low_b.at[i], part_slots[part])

    def down_part(part):
        i = part // 2
        if part % 2 == 0:
            return going(1, part_source(part, 0), high_a.at[i], part_slots[part])
        return going(1, down_b.at[i], high_b.at[i], part_slots[part])

    def pack(g):
        load(g).wait()
        slot = lax.rem(g, SLOTS)
        for k in range(GROUP):
            rows = slice(RADIUS * k, RADIUS * (k + 1))
            send_up[slot, rows, :] = v[g * GROUP + k, 1 : RADIUS + 1, :]
            send_down[slot, rows, :] = v[g * GROUP + k, 0:RADIUS, :]

    def y_each(g, do, sending, ways=(up, down)):
        @pl.when(has_high if sending else has_low)
        def _():
            do(ways[0](g))

        @pl.when(has_low if sending else has_high)
        def _():
            do(ways[1](g))

    in_parts = (up_part, down_part)

    def pack_second(i):
        g = i * last
        load(g).wait()
        for k in range(GROUP):
            rows = slice(SECOND * k, SECOND * (k + 1))
            up_b[i, rows, :] = v[g * GROUP + k, 1 : SECOND + 1, :]
            down_b[i, rows, :] = v[g * GROUP + k, FIRST : FIRST + SECOND, :]

    def y_start(g):
        y_each(g, lambda c: c.start(), True)

    def y_wait_send(g):
        y_each(g, lambda c: c.wait_send(), True)

    def y_wait_recv(g):
        y_each(g, lambda c: c.wait_recv(), False)

    neighbours = sum(jnp.where(there, 1, 0) for there in (has_low, has_high, has_prev, has_next))
    pl.semaphore_wait(barrier, neighbours)
    y_each(0, lambda c: c.start(), True, in_parts)
    pack_second(0)
    y_each(1, lambda c: c.start(), True, in_parts)
    pack(1)
    y_start(1)
    for g in range(2, SLOTS + 1):
        pack(g)
    pack_second(1)
    for copy in small[:5]:
        copy.wait()

    @pl.when(jnp.logical_not(has_low))
    def _():
        @pl.loop(0, last - 1)
        def _(g):
            got_low[g] = jnp.zeros((PACKED, cols), F32)

        low_a[...] = jnp.zeros(low_a.shape, F32)
        low_b[...] = jnp.zeros(low_b.shape, F32)

    @pl.when(jnp.logical_not(has_high))
    def _():
        @pl.loop(0, last - 1)
        def _(g):
            got_high[g] = jnp.zeros((PACKED, cols), F32)

        high_a[...] = jnp.zeros(high_a.shape, F32)
        high_b[...] = jnp.zeros(high_b.shape, F32)

    for there, side in ((has_prev, 0), (has_next, 2)):

        @pl.when(jnp.logical_not(there))
        def _(side=side):
            @pl.loop(0, groups)
            def _(g):
                @pl.loop(0, temp_rows)
                def _(t):
                    xt[g, t, side * GROUP : (side + 1) * GROUP, :] = jnp.zeros((GROUP, cols), F32)

    wide = GROUP * temp_rows

    def temperature(high_ref, low_ref, width, blocks):
        t_of = iota((temp_rows, width), 0)
        col = iota((temp_rows, width), 1)
        col8 = iota((GROUP, width), 1)
        index = jnp.full(col.shape, -1, jnp.int32)
        k_of = jnp.full(col8.shape, -1, jnp.int32)
        for q0, per, tap in blocks:
            k = count_steps(col - q0, per, GROUP - 1)
            here = (col >= q0) & (col < q0 + GROUP * per)
            index = jnp.where(here, col - q0 - per * k + tap - t_of, index)
            here = (col8 >= q0) & (col8 < q0 + GROUP * per)
            k_of = jnp.where(here, count_steps(col8 - q0, per, GROUP - 1), k_of)
        found = lookup(temp_taps, index)
        same = k_of == iota((GROUP, width), 0)
        for t in range(0, temp_rows, 2):
            block = jnp.concatenate(
                [jnp.where(same, found[t + i : t + i + 1, :], 0.0) for i in range(2)], axis=0
            )
            high, low = halves(block)
            high_ref[t * GROUP : (t + 2) * GROUP, :] = high
            low_ref[t * GROUP : (t + 2) * GROUP, :] = low

    for m, per, tap in ((0, temp_rows, RADIUS), (1, RADIUS, 0), (2, RADIUS, TAPS)):
        temperature(a_mats.at[2 * m], a_mats.at[2 * m + 1], wide, ((0, per, tap),))
    for m, tap in ((0, SECOND), (1, TAPS)):
        temperature(a_tail.at[2 * m], a_tail.at[2 * m + 1], GROUP * FIRST, ((0, FIRST, tap),))
    temperature(
        a_final.at[0],
        a_final.at[1],
        a_final.shape[2],
        ((0, SECOND, 0), (GROUP * SECOND, SECOND, TAPS + FIRST)),
    )

    lane = iota((GROUP, cols), 1)
    source = lane & 15
    for s in range(cols // 16):
        source = source + jnp.where((lane >> 4) == s, jump_table[s] * 16, 0)

    @pl.loop(0, cols // 16)
    def _(i):
        row = iota((16, cols), 0) + i * 16
        hot = row == jnp.concatenate([source, source], axis=0)
        jump_mat[pl.ds(pl.multiple_of(i * 16, 16), 16), :] = jnp.where(hot, 1.0, 0.0).astype(BF16)

    for copy in small[5:]:
        copy.wait()
    choices = fu.shape[0]
    band = iw.shape[1] // choices
    span = w2.shape[1]
    w2[...] = jnp.zeros(w2.shape, F32)
    for kb in range(groups):
        for j in range(choices):
            w2[(kb * choices + j) * GROUP : (kb * choices + j + 1) * GROUP, 0:band] = iw[
                kb * GROUP : (kb + 1) * GROUP, j * band : (j + 1) * band
            ]
    offset = band_start[0] - p * cap_rows + cap_rows // 2
    place_row = iota((span, span), 0)
    place_col = iota((span, span), 1)
    place = jnp.where((place_col == place_row + offset) & (place_row < band), 1.0, 0.0)
    w2p[...] = DISCOUNT * jnp.dot(
        w2[...], place, precision=lax.Precision.HIGHEST, preferred_element_type=F32
    )

    def landing_matrix(width, blocks):
        def columns(q):
            row = jnp.full(q.shape, -1000, jnp.int32)
            for q0, first, count in blocks:
                row = jnp.where(q >= q0, stacked_map(q - q0, first, count), row)
            return row

        parts = []
        for e0 in range(0, span, 32):
            e = iota((32, width), 0) + e0
            q = iota((32, width), 1)
            parts.append(lookup(cap_taps, columns(q) - e - 1))
        full = jnp.dot(
            w2p[...],
            jnp.concatenate(parts, axis=0),
            precision=lax.Precision.HIGHEST,
            preferred_element_type=F32,
        )
        high = rounded(full)
        q = iota(full.shape, 1)
        low_part = q < 0
        for q0, first, count in blocks:
            n = count * 3 * GROUP
            low_part = low_part | ((q >= q0 + 2 * n) & (q < q0 + 3 * n))
        return jnp.where(low_part, full - high, high)

    ext0 = 9 * GROUP * FIRST_PASS
    g_late[...] = landing_matrix(
        WIDE, tuple((i * BLOCK, EARLY + i, 1) for i in range(groups - EARLY))
    ).astype(BF16)
    g_second[...] = landing_matrix(WIDE, ((0, FIRST_PASS, EARLY - FIRST_PASS),)).astype(BF16)
    w2e = landing_matrix(WIDE, ((0, 0, FIRST_PASS),))
    elane = iota((GROUP, WIDE), 1)
    eye = jnp.where(iota((cap_rows, cap_rows), 0) == iota((cap_rows, cap_rows), 1), 1.0, 0.0)

    def turned(x):
        return lax.dot_general(
            eye,
            x,
            (((1,), (1,)), ((), ())),
            precision=lax.Precision.HIGHEST,
            preferred_element_type=F32,
        )

    flows = turned(fu[...])
    numbers = turned(ci[...].astype(F32))
    for kb in range(groups):
        for j0 in range(0, choices, 2):
            pair = []
            for j in (j0, j0 + 1):
                at = (kb * choices + j) * GROUP
                piece = w2e[at : at + GROUP, :]
                flow = flows[kb * GROUP : (kb + 1) * GROUP, j : j + 1]
                number = numbers[kb * GROUP : (kb + 1) * GROUP, j : j + 1]
                square = number * number
                f1 = rounded(flow)
                f2 = rounded(flow - f1)
                f3 = flow - f1 - f2
                q1 = rounded(square)
                q2 = square - q1
                for i, value in enumerate(
                    (f1, f2, f3, number, number, number, -q1, -q1, -q1, -q2, -q2, -q2)
                ):
                    piece = jnp.where(elane == ext0 + i, value, piece)
                pair.append(piece)
            at = (kb * choices + j0) * GROUP
            g_early[at : at + 2 * GROUP, :] = jnp.concatenate(pair, axis=0).astype(BF16)
    gain_row = gain[...].reshape(1, cols) * (1.0 / (LEVELS - 1))
    g1 = rounded(gain_row)
    g2 = rounded(gain_row - g1)
    g3 = gain_row - g1 - g2
    ext_count = WIDE - ext0
    erow = iota((ext_count, cols), 0)
    base = jnp.where(erow < 3, 1.0, 0.0)
    for i, value in enumerate((g1, g2, g3)):
        base = jnp.where(erow == 3 + i, value, base)
    ext_base[...] = base

    parts = temp_rows // GROUP

    def k_copy(g, ts, slot, to_next):
        src = xt.at[g, ts, GROUP : 2 * GROUP, :]
        side = 0 if to_next else 2
        return pltpu.make_async_remote_copy(
            src_ref=src,
            dst_ref=xt.at[g, ts, side * GROUP : (side + 1) * GROUP, :],
            send_sem=k_sent.at[0 if to_next else 1, slot],
            recv_sem=k_recv.at[0 if to_next else 1, slot],
            device_id={"cap": p + 1 if to_next else p - 1},
            device_id_type=MESH,
        )

    def k_each(g, ts, slot, do, sending):
        @pl.when(has_next if sending else has_prev)
        def _():
            do(k_copy(g, ts, slot, True))

        @pl.when(has_prev if sending else has_next)
        def _():
            do(k_copy(g, ts, slot, False))

    odd = lax.rem(p, 2) == 1
    even = lax.rem(p, 2) == 0

    def k_send(g, ts, slot):
        for there, to_next in (
            (odd & has_next, True),
            (even & has_prev, False),
            (even & has_next, True),
            (odd & has_prev, False),
        ):

            @pl.when(there)
            def _(to_next=to_next):
                k_copy(g, ts, slot, to_next).start()

    every = pl.ds(0, temp_rows)

    def k_start(g):
        k_send(g, every, g)

    def k_wait_recv(g):
        k_each(g, every, g, lambda c: c.wait_recv(), False)

    def k_wait_send(g):
        k_each(g, every, g, lambda c: c.wait_send(), True)

    def part_rows(i):
        return pl.ds(pl.multiple_of(i * GROUP, GROUP), GROUP)

    def term(high_ref, low_ref, rows, x):
        high, low = halves(x)
        a = high_ref[rows, :]
        return mm(a, high) + mm(a, low) + mm(low_ref[rows, :], high)

    def own_term(g):
        x = v[pl.ds(g * GROUP, GROUP)].reshape(wide, cols)
        return term(a_mats.at[0], a_mats.at[1], slice(None), x)

    def mix(g, total, ts):
        high, low = halves(total)
        jumped = mm(high, jump_mat[...]) + mm(low, jump_mat[...])
        for i, t in enumerate(ts):
            rows = slice(i * GROUP, (i + 1) * GROUP)
            h = hazard[t]
            xt[g, t, GROUP : 2 * GROUP, :] = (1.0 - h) * total[rows] + h * jumped[rows]

    def first_part(i, own, lo, hi):
        rows = slice(lo * GROUP, hi * GROUP)
        return (
            own[rows]
            + term(a_tail.at[0], a_tail.at[1], rows, low_a[i].reshape(GROUP * FIRST, cols))
            + term(a_tail.at[2], a_tail.at[3], rows, high_a[i].reshape(GROUP * FIRST, cols))
        )

    def second_part(i, blocks):
        pad = jnp.zeros((a_final.shape[2] - 2 * GROUP * SECOND, cols), F32)
        x = jnp.concatenate([low_b[i], high_b[i], pad], axis=0)
        sums = []
        for lo, hi in blocks:
            sums.append(term(a_final.at[0], a_final.at[1], slice(lo * GROUP, hi * GROUP), x))
        return jnp.concatenate(sums, axis=0)

    def y_step(g):
        pad = jnp.zeros((wide - PACKED, cols), F32)
        total = own_term(g)
        y_wait_recv(g)
        for m, got in ((1, got_low), (2, got_high)):
            x = jnp.concatenate([got[g - 1], pad], axis=0)
            total = total + term(a_mats.at[2 * m], a_mats.at[2 * m + 1], slice(None), x)
        mix(g, total, range(temp_rows))

    def stacked(first_group, count, t):
        x = jnp.concatenate([xt[first_group + i, t] for i in range(count)], axis=0)
        high = rounded(x)
        return [high, x - high, high]

    def early(pair):
        sides = []
        for i in range(2):
            t = pair * 2 + i
            cost = jnp.full((ext_count, cols), temp_cost[t] * (1.0 / ((LEVELS - 1) * (LEVELS - 1))), F32)
            c1 = rounded(cost)
            c2 = rounded(cost - c1)
            c3 = cost - c1 - c2
            ext = ext_base[...]
            for r, value in enumerate((c1, c2, c3, c1, c2, c3)):
                ext = jnp.where(erow == 6 + r, value, ext)
            sides.append(jnp.concatenate(stacked(0, FIRST_PASS, t) + [ext], axis=0).astype(BF16))
        both = jnp.concatenate(sides, axis=1)
        for n in range(3):
            acc[pair, n] = mm(g_early[...], both[:, n * 256 : (n + 1) * 256])

    def second(pair):
        count = EARLY - FIRST_PASS
        pad = jnp.zeros((WIDE - 9 * GROUP * count, cols), F32)
        sides = []
        for i in range(2):
            rows = stacked(FIRST_PASS, count, pair * 2 + i) + [pad]
            sides.append(jnp.concatenate(rows, axis=0).astype(BF16))
        both = jnp.concatenate(sides, axis=1)
        for n in range(3):
            acc[pair, n] += mm(g_second[...], both[:, n * 256 : (n + 1) * 256])

    def build(g, pair):
        pad = jnp.zeros((BLOCK - 9 * GROUP, cols), F32)
        rows = slice((g - EARLY) * BLOCK, (g - EARLY + 1) * BLOCK)
        for i in range(2):
            rhs_late[pair, rows, i * cols : (i + 1) * cols] = jnp.concatenate(
                stacked(g, 1, pair * 2 + i) + [pad], axis=0
            ).astype(BF16)

    def late(pair, half, slot):
        pad = jnp.zeros((WIDE - (last - EARLY) * BLOCK - 9 * GROUP, cols), F32)
        final = jnp.concatenate(
            [
                jnp.concatenate(stacked(last, 1, pair * 2 + i) + [pad], axis=0).astype(BF16)
                for i in range(2)
            ],
            axis=1,
        )
        both = jnp.concatenate([rhs_late[pair], final], axis=0)
        for n in range(3):
            score = acc[pair, n] + mm(g_late[...], both[:, n * 256 : (n + 1) * 256])
            best = jnp.max(score.reshape(groups, choices, GROUP, 256), axis=1).reshape(cap_rows, 256)
            if n == 0:
                stage[half, slot, :, 0:256] = best
            elif n == 1:
                stage[half, slot, :, 256:384] = best[:, 0:128]
                stage[half, slot + 1, :, 0:128] = best[:, 128:256]
            else:
                stage[half, slot + 1, :, 128:384] = best

    pairs = temp_rows // 2

    def pair_loop(lo, hi, do):
        @pl.loop(lo, hi, step=2)
        def _(pair):
            do(pair)
            do(pair + 1)

    own = own_term(0)
    for part in range(2):
        y_each(part, lambda c: c.wait_send(), True, in_parts)
    y_start(2)
    for part in range(2):
        y_each(part, lambda c: c.wait_recv(), False, in_parts)
    everywhere = (0, temp_rows)
    mix(0, first_part(0, own, *everywhere) + second_part(0, (everywhere,)), range(temp_rows))
    k_start(0)

    def y_turn(g):
        y_wait_send(g)
        y_start(g + 2)
        y_step(g)
        k_start(g)

    @pl.loop(1, FIRST_PASS)
    def _(g):
        y_turn(g)
        pack(g + SLOTS)

    for done in range(FIRST_PASS):
        if done == FIRST_PASS - 1:
            y_turn(FIRST_PASS)
        k_wait_recv(done)
    pair_loop(0, pairs // 2, early)
    y_turn(EARLY - 1)
    pair_loop(pairs // 2, pairs, early)

    y_wait_send(EARLY)
    y_each(2, lambda c: c.start(), True, in_parts)
    y_step(EARLY)
    k_start(EARLY)
    for done in range(FIRST_PASS, EARLY):
        k_wait_recv(done)
    pair_loop(0, 10, second)
    y_wait_send(EARLY + 1)
    y_step(EARLY + 1)
    k_start(EARLY + 1)
    pair_loop(10, pairs, second)
    y_each(3, lambda c: c.start(), True, in_parts)
    k_wait_recv(EARLY)
    pair_loop(0, pairs, functools.partial(build, EARLY))

    def k_part(i):
        k_send(last, part_rows(i), last + i)

    own = own_term(last)
    y_each(2, lambda c: c.wait_recv(), False, in_parts)
    mix(last, first_part(1, own, 8, 24), range(8, 24))
    k_part(1)
    k_part(2)
    outer = jnp.concatenate([first_part(1, own, 24, 32), first_part(1, own, 0, 8)], axis=0)
    y_each(3, lambda c: c.wait_recv(), False, in_parts)
    mix(last, outer + second_part(1, ((24, 32), (0, 8))), (*range(24, 32), *range(8)))
    k_part(3)
    k_part(0)

    k_wait_recv(EARLY + 1)
    pair_loop(0, pairs, functools.partial(build, EARLY + 1))

    def octet(step):
        return lax.rem(step + 1, parts)

    def land(step):
        i = octet(step)
        k_each(last, part_rows(i), last + i, lambda c: c.wait_recv(), False)
        for slot in range(0, GROUP, 2):
            late(i * (GROUP // 2) + slot // 2, lax.rem(step, 2), slot)

    def turn(step):
        rows = part_rows(octet(step))
        half = lax.rem(step, 2)
        for kb in range(groups):
            at = slice(kb * GROUP, (kb + 1) * GROUP)
            out[at, rows, :] = jnp.swapaxes(stage[half, :, at, :], 0, 1)

    land(0)

    @pl.loop(1, parts)
    def _(step):
        land(step)
        turn(step - 1)

    turn(parts - 1)

    for part in range(2, 4):
        y_each(part, lambda c: c.wait_send(), True, in_parts)
    for g in range(last):
        k_wait_send(g)
    for i in range(parts):
        k_each(last, part_rows(i), last + i, lambda c: c.wait_send(), True)


def per_device(n_cap, n_temp, *args):
    value_next, interp_weights = args[0], args[6]
    cap_rows, temp_rows, cols = value_next.shape
    args = list(args)
    args[7], args[8] = args[7].T, args[8].T
    args[0] = pltpu.with_memory_space_constraint(value_next, pltpu.HBM)
    choices = args[8].shape[0]
    groups = cap_rows // GROUP
    rows = cap_rows * choices
    parts = temp_rows // GROUP
    hbm = pl.BlockSpec(memory_space=pl.ANY)
    return pl.pallas_call(
        functools.partial(kernel, n_cap, n_temp),
        out_shape=pltpu.VMEM(value_next.shape, F32),
        in_specs=[hbm] * 5 + [pl.BlockSpec(memory_space=pltpu.SMEM)] + [hbm] * 5,
        out_specs=pl.BlockSpec(memory_space=pltpu.VMEM),
        scratch_shapes=[
            *(pltpu.SMEM(args[i].shape, args[i].dtype) for i in (1, 2, 3, 4)),
            pltpu.SMEM(args[10].shape, F32),
            pltpu.VMEM((cap_rows, temp_rows, cols), F32),
            pltpu.VMEM((SLOTS, PACKED, cols), F32),
            pltpu.VMEM((SLOTS, PACKED, cols), F32),
            pltpu.VMEM((groups - 2, PACKED, cols), F32),
            pltpu.VMEM((groups - 2, PACKED, cols), F32),
            pltpu.VMEM((2, GROUP, FIRST, cols), F32),
            pltpu.VMEM((2, GROUP, FIRST, cols), F32),
            *(pltpu.VMEM((2, GROUP * SECOND, cols), F32) for _ in range(4)),
            pltpu.VMEM((groups, temp_rows, 3 * GROUP, cols), F32),
            pltpu.VMEM((temp_rows // 2, 3, rows, 256), F32),
            pltpu.VMEM((2, GROUP, cap_rows, cols), F32),
            pltpu.VMEM(interp_weights.shape, F32),
            pltpu.VMEM((choices, cap_rows), jnp.int32),
            pltpu.VMEM((choices, cap_rows), F32),
            pltpu.VMEM((cols,), F32),
            pltpu.VMEM((6, GROUP * temp_rows, GROUP * temp_rows), BF16),
            pltpu.VMEM((4, GROUP * temp_rows, GROUP * FIRST), BF16),
            pltpu.VMEM((2, GROUP * temp_rows, 128), BF16),
            pltpu.VMEM((cols, cols), BF16),
            pltpu.VMEM((rows, 128), F32),
            pltpu.VMEM((rows, 128), F32),
            pltpu.VMEM((rows, WIDE), BF16),
            pltpu.VMEM((rows, WIDE), BF16),
            pltpu.VMEM((rows, WIDE), BF16),
            pltpu.VMEM((temp_rows // 2, (groups - 1 - EARLY) * BLOCK, 2 * cols), BF16),
            pltpu.VMEM((WIDE - 9 * GROUP * FIRST_PASS, cols), F32),
            pltpu.SemaphoreType.DMA((groups + 9,)),
            pltpu.SemaphoreType.DMA((2, groups + 2)),
            pltpu.SemaphoreType.DMA((2, groups + 2)),
            pltpu.SemaphoreType.DMA((2, groups - 1 + parts)),
            pltpu.SemaphoreType.DMA((2, groups - 1 + parts)),
        ],
        compiler_params=pltpu.CompilerParams(
            collective_id=0, has_side_effects=True, vmem_limit_bytes=58 * 1024 * 1024
        ),
        cost_estimate=pl.CostEstimate(flops=6_000_000_000, bytes_accessed=8_000_000, transcendentals=0),
    )(*args)


def solution(mesh):
    in_specs = (
        P("cap", "temp", None),
        P(),
        P(),
        P("temp"),
        P(),
        P("cap"),
        P("cap", None),
        P("cap", None),
        P("cap", None),
        P(),
        P("temp"),
    )
    return jax.shard_map(
        functools.partial(per_device, mesh.shape["cap"], mesh.shape["temp"]),
        mesh=mesh,
        in_specs=in_specs,
        out_specs=P("cap", "temp", None),
        check_vma=False,
    )
```
